32 devices in a mesh: blk: 16 (over z, y, core), grp: 2 (over x).
Axes of the slice: x: 2, y: 2, z: 4, core: 2. Of those that a mesh axis runs over, the one named last changes fastest.
Arguments:
- queries: bfloat16 [8192, 2048], P(('blk', 'grp')), may hold values from -100 to 100
- keys: bfloat16 [8192, 1024], P(('blk', 'grp')), may hold values from -4 to 4
- values: bfloat16 [8192, 1024], P(('blk', 'grp')), may hold values from -6 to 6
Outputs:
- attended: bfloat16 [8192, 2048], P(('blk', 'grp'))
The draws below stay inside these ranges and needn't reach their ends.
All inputs are finite; a program needn't handle non-finite values.
Results may differ from the reference program's by a relative error of at most 0.0049.
Values may be sent and summed in bfloat16 or wider, within the bound.
A program may use at most 64 MiB of HBM per device.

```python
import jax
import jax.numpy as jnp
from jax import lax

HEADS = 16
KV_HEADS = 8
HEAD_DIM = 128
WINDOW = 1024
TOK_DEV = 256
TOKENS = 8192


def paired_draws(key):
    base_keys = jnp.clip(jax.random.normal(jax.random.fold_in(key, 11), (TOKENS, KV_HEADS * HEAD_DIM), jnp.float32), -3.0, 3.0)
    base_queries = jnp.clip(jax.random.normal(jax.random.fold_in(key, 12), (TOKENS, HEADS * HEAD_DIM), jnp.float32), -3.0, 3.0)
    return (base_queries, base_keys)


def draw_queries(key, part):
    return paired_draws(key)[0].astype(jnp.bfloat16)


def draw_keys(key, part):
    return paired_draws(key)[1].astype(jnp.bfloat16)


def level_of(rng, dims, cuts, smallest, top_value):
    def one(axis_at, blocks):
        draws = jax.random.uniform(jax.random.fold_in(jax.random.fold_in(rng, 6), axis_at), (blocks,), jnp.float32, smallest / len(cuts), top_value / len(cuts))
        return jnp.repeat(jnp.exp(draws), dims[axis_at] // blocks).reshape((-1,) + (1,) * (len(dims) - axis_at - 1))

    factor_of = one(*cuts[0])
    for cut in cuts[1:]:
        factor_of = factor_of * one(*cut)
    return factor_of


def gaussian(rng, extent, width, limit, split=(), kind=jnp.bfloat16):
    drawn = width * jax.random.normal(rng, extent, jnp.float32)
    if split:
        drawn = drawn * level_of(rng, extent, split, -0.22, 0.18)
    return jnp.clip(drawn, -limit, limit).astype(kind)


def setup_inputs(seed: int = 0) -> dict:
    streams_of = jax.random.split(jax.random.key(seed), 4)
    return {
        "queries": draw_queries(jax.random.fold_in(streams_of[3], 71), 0),
        "keys": draw_keys(jax.random.fold_in(streams_of[3], 71), 0),
        "values": gaussian(streams_of[2], (TOKENS, KV_HEADS * HEAD_DIM), 1.0, 6.0, ((0, 32),)),
    }


def attend_block(query_rows, key_win, value_win, block_index):
    tok_rows = query_rows.shape[0]
    group_size = HEADS // KV_HEADS
    span_rows = key_win.shape[0]
    row_ids = jnp.arange(tok_rows, dtype=jnp.int32)[:, None]
    col_ids = jnp.arange(span_rows, dtype=jnp.int32)[None, :]
    position = block_index * tok_rows - WINDOW + col_ids
    allowed = (col_ids > row_ids) & (col_ids <= row_ids + WINDOW) & (position >= 0)

    def head_group(head_index):
        query_part = lax.dynamic_slice_in_dim(query_rows, head_index * group_size * HEAD_DIM, group_size * HEAD_DIM, 1)
        query_part = query_part.reshape(tok_rows, group_size, HEAD_DIM).astype(jnp.float32)
        key_part = lax.dynamic_slice_in_dim(key_win, head_index * HEAD_DIM, HEAD_DIM, 1).astype(jnp.float32)
        value_part = lax.dynamic_slice_in_dim(value_win, head_index * HEAD_DIM, HEAD_DIM, 1).astype(jnp.float32)
        score = jnp.einsum('thd,kd->htk', query_part, key_part) * (HEAD_DIM ** -0.5)
        score = jnp.where(allowed[None], score, jnp.float32(-1e30))
        largest = jnp.max(score, axis=2, keepdims=True)
        expo = jnp.where(allowed[None], jnp.exp(score - largest), jnp.float32(0.0))
        total = jnp.sum(expo, axis=2, keepdims=True)
        weight = (expo / total).astype(jnp.bfloat16)
        output = jnp.einsum('htk,kd->thd', weight.astype(jnp.float32), value_part)
        return output.astype(jnp.bfloat16).reshape(tok_rows, group_size * HEAD_DIM)

    parts = lax.map(head_group, jnp.arange(KV_HEADS, dtype=jnp.int32))
    return jnp.transpose(parts, (1, 0, 2)).reshape(tok_rows, HEADS * HEAD_DIM)


def reference(queries, keys, values):
    padding = jnp.zeros((WINDOW, keys.shape[1]), keys.dtype)
    key_pad = jnp.concatenate([padding, keys], axis=0)
    value_pad = jnp.concatenate([padding, values], axis=0)

    def one_block(block_index):
        start_row = (block_index * TOK_DEV).astype(jnp.int32)
        query_rows = lax.dynamic_slice_in_dim(queries, start_row, TOK_DEV, 0)
        key_win = lax.dynamic_slice_in_dim(key_pad, start_row, WINDOW + TOK_DEV, 0)
        value_win = lax.dynamic_slice_in_dim(value_pad, start_row, WINDOW + TOK_DEV, 0)
        return attend_block(query_rows, key_win, value_win, block_index)

    blocks = lax.map(one_block, jnp.arange(TOKENS // TOK_DEV, dtype=jnp.int32))
    return blocks.reshape(TOKENS, HEADS * HEAD_DIM)
```

```python
import functools

import jax
import jax.numpy as jnp
from jax import lax
from jax.experimental import pallas as pl
from jax.experimental.pallas import tpu as pltpu
from jax.sharding import PartitionSpec as P

HEADS = 16
KV_HEADS = 8
HEAD_DIM = 128
WINDOW = 1024
GROUP = HEADS // KV_HEADS
HALF_KV = KV_HEADS // 2
SLOTS = 7
SCALE_LOG2E = HEAD_DIM ** -0.5 * 1.4426950408889634
MESH = pl.DeviceIdType.MESH


def fused_kernel(
    rows, q_ref, k_ref, v_ref, o_ref, kv, other, qbuf, obuf,
    stage_sem, qstage_sem, qsend, qrecv, send, recv, osem, osend, orecv,
):
    blk = lax.axis_index("blk")
    side = lax.axis_index("grp")
    row = blk // 2
    core = blk % 2
    tok = q_ref.shape[0]
    has_prev = row > 0
    has_next = row < rows - 1
    own_slot = 4 + 2 * core

    partner = (2 * row + 1 - core, side)
    next_same = (2 * row + 2 + core, side)
    next_cross = (2 * row + 3 - core, side)
    side_same = (2 * row + core, 1 - side)
    side_cross = (2 * row + 1 - core, 1 - side)
    prev_same = (2 * row - 2 + core, side)
    prev_cross = (2 * row - 1 - core, side)

    def cols(index, width):
        return pl.ds(pl.multiple_of(index * width, width), width)

    def stage(j):
        mine = cols(core * HALF_KV + j, HEAD_DIM)
        rest = cols((1 - core) * HALF_KV + j, HEAD_DIM)
        return [
            pltpu.make_async_copy(k_ref.at[:, rest], other.at[j, 0], stage_sem.at[j, 0]),
            pltpu.make_async_copy(v_ref.at[:, rest], other.at[j, 1], stage_sem.at[j, 1]),
            pltpu.make_async_copy(k_ref.at[:, mine], kv.at[own_slot, j, 0], stage_sem.at[j, 2]),
            pltpu.make_async_copy(v_ref.at[:, mine], kv.at[own_slot, j, 1], stage_sem.at[j, 3]),
        ]

    def q_stage(j):
        mine = cols(core * HALF_KV + j, GROUP * HEAD_DIM)
        return pltpu.make_async_copy(q_ref.at[:, mine], qbuf.at[core, j], qstage_sem.at[j])

    def q_swap(j, block):
        rest = cols((1 - core) * HALF_KV + j, GROUP * HEAD_DIM)
        return pltpu.make_async_remote_copy(
            src_ref=q_ref.at[:, rest], dst_ref=qbuf.at[block, j],
            send_sem=qsend.at[j], recv_sem=qrecv.at[j], device_id=partner, device_id_type=MESH,
        )

    def remote(src, dst, kind, arrival, j, device):
        return pltpu.make_async_remote_copy(
            src_ref=src, dst_ref=dst, send_sem=send.at[kind, j], recv_sem=recv.at[arrival, j],
            device_id=device, device_id_type=MESH,
        )

    def to_partner(j):
        return remote(other.at[j], kv.at[own_slot, j], 0, own_slot, j, partner)

    def to_next(j):
        return [
            remote(kv.at[own_slot, j], kv.at[2 * core, j], 1, 2 * core, j, next_same),
            remote(other.at[j], kv.at[2 * core, j], 2, 2 * core, j, next_cross),
        ]

    def to_side(j):
        slot = jnp.where(side == 0, 3 + 2 * core, 5)
        return [
            remote(kv.at[own_slot, j], kv.at[slot, j], 3, slot, j, side_same),
            remote(other.at[j], kv.at[slot, j], 4, slot, j, side_cross),
        ]

    sends_side = jnp.logical_or(side == 0, core == 0)

    def pass_side_keys(j, slot, kind):
        return remote(kv.at[slot, j, 0], kv.at[1, j, 0], kind, 1, j, side_same)

    def pass_side_whole(j):
        return remote(kv.at[2, j], kv.at[3, j], 5, 3, j, side_same)

    def pass_next_values(j):
        return remote(kv.at[5, j, 1], kv.at[1, j, 1], 6, 7, j, next_same)

    def arrived(slot, j):
        remote(kv.at[slot, j], kv.at[slot, j], 0, slot, j, partner).wait_recv()

    def arrived_part(part, arrival, j):
        remote(kv.at[1, j, part], kv.at[1, j, part], 0, arrival, j, partner).wait_recv()

    def send_direct(j):
        for copy in stage(j):
            copy.wait()
        to_partner(j).start()

        @pl.when(sends_side)
        def _():
            for copy in to_side(j):
                copy.start()

        @pl.when(has_next)
        def _():
            for copy in to_next(j):
                copy.start()

    def forward(j):
        @pl.when(has_prev)
        def _():
            arrived(2, j)

            @pl.when(side == 1)
            def _():
                pass_side_whole(j).start()
                arrived(0, j)
                pass_side_keys(j, 0, 7).start()

            @pl.when(side == 0)
            def _():
                pass_side_keys(j, 2, 5).start()
                arrived(0, j)

        arrived(5, j)

        @pl.when(has_next)
        def _():
            pass_next_values(j).start()

    def await_rest(j):
        q_stage(j).wait()
        q_swap(j, 1 - core).wait_recv()
        arrived(6 - 2 * core, j)

        @pl.when(jnp.logical_or(side == 1, has_prev))
        def _():
            arrived(3, j)

        @pl.when(has_prev)
        def _():
            arrived_part(0, 1, j)
            arrived_part(1, 7, j)

    def attend(j, masked):
        upper = (
            lax.broadcasted_iota(jnp.int32, (tok, tok), 1) > lax.broadcasted_iota(jnp.int32, (tok, tok), 0)
        )

        def one_block(block, carry):
            base = 2 * block
            for h in range(GROUP):
                q = qbuf[block, j, :, h * HEAD_DIM:(h + 1) * HEAD_DIM]
                score = []
                for i in range(5):
                    s = lax.dot_general(
                        q, kv[base + i, j, 0], (((1,), (1,)), ((), ())), preferred_element_type=jnp.float32
                    )
                    if masked and i < 4:
                        s = jnp.where(4 * row + side + base + i >= 4, s, jnp.float32(-1e30))
                    score.append(s)
                score = [jnp.where(upper, score[0], score[4])] + score[1:4]
                top = jnp.max(jnp.maximum(jnp.maximum(score[0], score[1]), jnp.maximum(score[2], score[3])),
                              axis=1, keepdims=True)
                expo = [jnp.exp2((s - top) * jnp.float32(SCALE_LOG2E)) for s in score]
                total = jnp.sum((expo[0] + expo[1]) + (expo[2] + expo[3]), axis=1, keepdims=True)
                zero = jnp.zeros_like(expo[0])
                weight = [jnp.where(upper, expo[0], zero)] + expo[1:] + [jnp.where(upper, zero, expo[0])]
                out = None
                for i in range(5):
                    term = jnp.dot(
                        weight[i].astype(jnp.bfloat16), kv[base + i, j, 1], preferred_element_type=jnp.float32
                    )
                    out = term if out is None else out + term
                obuf[block, j, :, h * HEAD_DIM:(h + 1) * HEAD_DIM] = (out * (1.0 / total)).astype(obuf.dtype)
            return carry

        lax.fori_loop(0, 2, one_block, 0)

    def out_local(j):
        return pltpu.make_async_copy(
            obuf.at[core, j], o_ref.at[:, cols(core * HALF_KV + j, GROUP * HEAD_DIM)], osem.at[j]
        )

    def out_remote(j, half):
        return pltpu.make_async_remote_copy(
            src_ref=obuf.at[1 - core, j], dst_ref=o_ref.at[:, cols(half * HALF_KV + j, GROUP * HEAD_DIM)],
            send_sem=osend.at[j], recv_sem=orecv.at[j], device_id=partner, device_id_type=MESH,
        )

    for j in range(HALF_KV):
        for copy in stage(j):
            copy.start()
        q_stage(j).start()

    barrier = pltpu.get_barrier_semaphore()
    for device in (partner, side_same, side_cross):
        pl.semaphore_signal(barrier, inc=1, device_id=device, device_id_type=MESH)

    @pl.when(has_next)
    def _():
        for device in (next_same, next_cross):
            pl.semaphore_signal(barrier, inc=1, device_id=device, device_id_type=MESH)

    @pl.when(has_prev)
    def _():
        for device in (prev_same, prev_cross):
            pl.semaphore_signal(barrier, inc=1, device_id=device, device_id_type=MESH)

    @pl.when(jnp.logical_not(has_prev))
    def _():
        kv[0:3] = jnp.zeros((3,) + kv.shape[1:], kv.dtype)

        @pl.when(side == 0)
        def _():
            kv[3] = jnp.zeros(kv.shape[1:], kv.dtype)

    pl.semaphore_wait(barrier, 3 + jnp.where(has_next, 2, 0) + jnp.where(has_prev, 2, 0))

    send_direct(0)
    send_direct(1)
    for j in range(HALF_KV):
        q_swap(j, core).start()

    def step(t, carry):
        @pl.when(t < HALF_KV)
        def _():
            forward(t)

        @pl.when(t < HALF_KV - 2)
        def _():
            send_direct(t + 2)

        @pl.when(t > 0)
        def _():
            j = t - 1
            await_rest(j)

            @pl.when(has_prev)
            def _():
                attend(j, False)

            @pl.when(jnp.logical_not(has_prev))
            def _():
                attend(j, True)

            out_remote(j, core).start()
            out_local(j).start()

        return carry

    lax.fori_loop(0, HALF_KV + 1, step, 0)

    def finish(j, carry):
        q_swap(j, core).wait_send()
        to_partner(j).wait_send()

        @pl.when(sends_side)
        def _():
            for copy in to_side(j):
                copy.wait_send()

        @pl.when(has_next)
        def _():
            for copy in to_next(j):
                copy.wait_send()
            pass_next_values(j).wait_send()

        @pl.when(has_prev)
        def _():
            @pl.when(side == 1)
            def _():
                pass_side_whole(j).wait_send()
                pass_side_keys(j, 0, 7).wait_send()

            @pl.when(side == 0)
            def _():
                pass_side_keys(j, 2, 5).wait_send()

        out_local(j).wait()
        out_remote(j, core).wait_send()
        out_remote(j, 1 - core).wait_recv()
        return carry

    lax.fori_loop(0, HALF_KV, finish, 0)


def fused_body(rows, queries, keys, values):
    tok = queries.shape[0]
    kind = queries.dtype
    wide = GROUP * HEAD_DIM
    dma = pltpu.SemaphoreType.DMA
    return pl.pallas_call(
        functools.partial(fused_kernel, rows),
        out_shape=jax.ShapeDtypeStruct(queries.shape, kind),
        in_specs=[pl.BlockSpec(memory_space=pl.ANY)] * 3,
        out_specs=pl.BlockSpec(memory_space=pl.ANY),
        scratch_shapes=[
            pltpu.VMEM((SLOTS, HALF_KV, 2, tok, HEAD_DIM), kind),
            pltpu.VMEM((HALF_KV, 2, tok, HEAD_DIM), kind),
            pltpu.VMEM((2, HALF_KV, tok, wide), kind),
            pltpu.VMEM((2, HALF_KV, tok, wide), kind),
            dma((HALF_KV, 4)),
            dma((HALF_KV,)),
            dma((HALF_KV,)),
            dma((HALF_KV,)),
            dma((8, HALF_KV)),
            dma((8, HALF_KV)),
            dma((HALF_KV,)),
            dma((HALF_KV,)),
            dma((HALF_KV,)),
        ],
        compiler_params=pltpu.CompilerParams(
            collective_id=0, has_side_effects=True, vmem_limit_bytes=48 * 1024 * 1024
        ),
        cost_estimate=pl.CostEstimate(
            flops=4 * tok * HEADS * HEAD_DIM * (WINDOW + tok), bytes_accessed=6 * tok * HEADS * HEAD_DIM,
            transcendentals=tok * HEADS * WINDOW,
        ),
        name="window_attention",
    )(queries, keys, values)


def from_behind(x, axis, by):
    peers = lax.axis_size(axis)
    pairs = [(i, i + by) for i in range(peers) if 0 <= i + by < peers]
    return lax.ppermute(x, axis, pairs)


def attend_block(query_rows, key_win, value_win, block_index):
    tok_rows = query_rows.shape[0]
    span_rows = key_win.shape[0]
    row_ids = jnp.arange(tok_rows, dtype=jnp.int32)[:, None]
    col_ids = jnp.arange(span_rows, dtype=jnp.int32)[None, :]
    position = block_index * tok_rows - WINDOW + col_ids
    allowed = (col_ids > row_ids) & (col_ids <= row_ids + WINDOW) & (position >= 0)

    def head_group(head_index):
        query_part = lax.dynamic_slice_in_dim(query_rows, head_index * GROUP * HEAD_DIM, GROUP * HEAD_DIM, 1)
        query_part = query_part.reshape(tok_rows, GROUP, HEAD_DIM)
        key_part = lax.dynamic_slice_in_dim(key_win, head_index * HEAD_DIM, HEAD_DIM, 1)
        value_part = lax.dynamic_slice_in_dim(value_win, head_index * HEAD_DIM, HEAD_DIM, 1)
        score = jnp.einsum(
            "thd,kd->htk", query_part, key_part, preferred_element_type=jnp.float32
        ) * HEAD_DIM ** (-0.5)
        score = jnp.where(allowed[None], score, jnp.float32(-1e30))
        largest = jnp.max(score, axis=2, keepdims=True)
        expo = jnp.where(allowed[None], jnp.exp(score - largest), jnp.float32(0.0))
        total = jnp.sum(expo, axis=2, keepdims=True)
        weight = (expo / total).astype(jnp.bfloat16)
        output = jnp.einsum("htk,kd->thd", weight, value_part, preferred_element_type=jnp.float32)
        return output.astype(jnp.bfloat16).reshape(tok_rows, GROUP * HEAD_DIM)

    parts = lax.map(head_group, jnp.arange(KV_HEADS, dtype=jnp.int32))
    return jnp.transpose(parts, (1, 0, 2)).reshape(tok_rows, HEADS * HEAD_DIM)


def plain_body(queries, keys, values):
    back_blocks = WINDOW // queries.shape[0]
    block_index = lax.axis_index(("blk", "grp"))
    pieces_k = []
    pieces_v = []
    for offset in range(back_blocks, 0, -1):
        moved_k, moved_v = from_behind((keys, values), ("blk", "grp"), offset)
        pieces_k.append(moved_k)
        pieces_v.append(moved_v)
    key_win = jnp.concatenate(pieces_k + [keys], axis=0)
    value_win = jnp.concatenate(pieces_v + [values], axis=0)
    return attend_block(queries, key_win, value_win, block_index)


def solution(mesh):
    blks, grps = mesh.shape["blk"], mesh.shape["grp"]
    placed = P(("blk", "grp"), None)

    def body(queries, keys, values):
        if grps == 2 and blks % 2 == 0 and 4 * queries.shape[0] == WINDOW:
            return fused_body(blks // 2, queries, keys, values)
        return plain_body(queries, keys, values)

    return jax.shard_map(
        body, mesh=mesh, in_specs=(placed, placed, placed), out_specs=placed, check_vma=False
    )
```

```python
import functools

import jax
import jax.numpy as jnp
from jax import lax
from jax.experimental import pallas as pl
from jax.experimental.pallas import tpu as pltpu
from jax.sharding import PartitionSpec as P

HEADS = 16
KV_HEADS = 8
HEAD_DIM = 128
WINDOW = 1024
GROUP = HEADS // KV_HEADS
HALF_KV = KV_HEADS // 2
SLOTS = 7
SCALE_LOG2E = HEAD_DIM ** -0.5 * 1.4426950408889634
MESH = pl.DeviceIdType.MESH


def fused_kernel(
    rows, q_ref, k_ref, v_ref, o_ref, kv, other, qbuf, obuf,
    stage_sem, qstage_sem, qsend, qrecv, send, recv, osem, osend, orecv,
):
    blk = lax.axis_index("blk")
    side = lax.axis_index("grp")
    row = blk // 2
    core = blk % 2
    tok = q_ref.shape[0]
    has_prev = row > 0
    has_next = row < rows - 1
    own_slot = 4 + 2 * core

    partner = (2 * row + 1 - core, side)
    next_same = (2 * row + 2 + core, side)
    next_cross = (2 * row + 3 - core, side)
    side_same = (2 * row + core, 1 - side)
    side_cross = (2 * row + 1 - core, 1 - side)
    prev_same = (2 * row - 2 + core, side)
    prev_cross = (2 * row - 1 - core, side)

    def cols(index, width):
        return pl.ds(pl.multiple_of(index * width, width), width)

    def stage(j, part, half):
        source = (k_ref, v_ref)[part].at[:, cols(half * HALF_KV + j, HEAD_DIM)]
        if half is core:
            return pltpu.make_async_copy(source, kv.at[own_slot, j, part], stage_sem.at[j, 2 + part])
        return pltpu.make_async_copy(source, other.at[j, part], stage_sem.at[j, part])

    def q_stage(j):
        mine = cols(core * HALF_KV + j, GROUP * HEAD_DIM)
        return pltpu.make_async_copy(q_ref.at[:, mine], qbuf.at[core, j], qstage_sem.at[j])

    def q_swap(j, block):
        rest = cols((1 - core) * HALF_KV + j, GROUP * HEAD_DIM)
        return pltpu.make_async_remote_copy(
            src_ref=q_ref.at[:, rest], dst_ref=qbuf.at[block, j],
            send_sem=qsend.at[j], recv_sem=qrecv.at[j], device_id=partner, device_id_type=MESH,
        )

    def remote(src, dst, kind, arrival, j, part, device):
        return pltpu.make_async_remote_copy(
            src_ref=src, dst_ref=dst, send_sem=send.at[kind, j, part], recv_sem=recv.at[arrival, j, part],
            device_id=device, device_id_type=MESH,
        )

    def piece(slot, j, part):
        return kv.at[slot, j, part]

    def to_partner(j, part):
        return remote(other.at[j, part], piece(own_slot, j, part), 0, own_slot, j, part, partner)

    def to_next(j, part):
        slot = 2 * core
        return [
            remote(piece(own_slot, j, part), piece(slot, j, part), 1, slot, j, part, next_same),
            remote(other.at[j, part], piece(slot, j, part), 2, slot, j, part, next_cross),
        ]

    def to_side(j, part):
        slot = jnp.where(side == 0, 3 + 2 * core, 5)
        return [
            remote(piece(own_slot, j, part), piece(slot, j, part), 3, slot, j, part, side_same),
            remote(other.at[j, part], piece(slot, j, part), 4, slot, j, part, side_cross),
        ]

    sends_side = jnp.logical_or(side == 0, core == 0)

    def pass_side(j, part, slot, to_slot, kind):
        return remote(piece(slot, j, part), piece(to_slot, j, part), kind, to_slot, j, part, side_same)

    def pass_next(j):
        return remote(piece(5, j, 1), piece(1, j, 1), 6, 1, j, 1, next_same)

    def arrived(slot, j, part):
        remote(piece(slot, j, part), piece(slot, j, part), 0, slot, j, part, partner).wait_recv()

    def direct(j, part, act):
        act(to_partner(j, part))

        @pl.when(sends_side)
        def _():
            for copy in to_side(j, part):
                act(copy)

        @pl.when(has_next)
        def _():
            for copy in to_next(j, part):
                act(copy)

    def forwards(j, part, act):
        @pl.when(jnp.logical_and(has_prev, side == 1))
        def _():
            act(pass_side(j, part, 2, 3, 5), 2)
            if part == 0:
                act(pass_side(j, part, 0, 1, 7), 0)
            else:
                act(None, 0)

        @pl.when(jnp.logical_and(has_prev, side == 0))
        def _():
            act(pass_side(j, part, 2, 1, 5) if part == 0 else None, 2)
            act(None, 0)

        if part == 0:
            act(None, 5)
        else:
            @pl.when(has_next)
            def _():
                act(pass_next(j), 5)

            @pl.when(jnp.logical_not(has_next))
            def _():
                act(None, 5)

    def start_direct(j, part):
        stage(j, part, core).wait()
        stage(j, part, 1 - core).wait()
        direct(j, part, lambda copy: copy.start())

    def exchange(j, part):
        def hand_on(copy, slot):
            arrived(slot, j, part)
            if copy is not None:
                copy.start()

        forwards(j, part, hand_on)
        direct(j, part, lambda copy: copy.wait_send())

        @pl.when(j < HALF_KV - 1)
        def _():
            start_direct(j + 1, part)

    def await_rest(j):
        q_stage(j).wait()
        q_swap(j, 1 - core).wait_recv()
        for part in (0, 1):
            arrived(6 - 2 * core, j, part)

            @pl.when(jnp.logical_or(side == 1, has_prev))
            def _():
                arrived(3, j, part)

            @pl.when(has_prev)
            def _():
                arrived(1, j, part)

    def attend(j, masked):
        upper = (
            lax.broadcasted_iota(jnp.int32, (tok, tok), 1) > lax.broadcasted_iota(jnp.int32, (tok, tok), 0)
        )

        def one_block(block, carry):
            base = 2 * block
            for h in range(GROUP):
                q = qbuf[block, j, :, h * HEAD_DIM:(h + 1) * HEAD_DIM]
                score = []
                for i in range(5):
                    s = lax.dot_general(
                        q, kv[base + i, j, 0], (((1,), (1,)), ((), ())), preferred_element_type=jnp.float32
                    )
                    if masked and i < 4:
                        s = jnp.where(4 * row + side + base + i >= 4, s, jnp.float32(-1e30))
                    score.append(s)
                score = [jnp.where(upper, score[0], score[4])] + score[1:4]
                top = jnp.max(jnp.maximum(jnp.maximum(score[0], score[1]), jnp.maximum(score[2], score[3])),
                              axis=1, keepdims=True)
                expo = [jnp.exp2((s - top) * jnp.float32(SCALE_LOG2E)) for s in score]
                total = jnp.sum((expo[0] + expo[1]) + (expo[2] + expo[3]), axis=1, keepdims=True)
                zero = jnp.zeros_like(expo[0])
                weight = [jnp.where(upper, expo[0], zero)] + expo[1:] + [jnp.where(upper, zero, expo[0])]
                out = None
                for i in range(5):
                    term = jnp.dot(
                        weight[i].astype(jnp.bfloat16), kv[base + i, j, 1], preferred_element_type=jnp.float32
                    )
                    out = term if out is None else out + term
                obuf[block, j, :, h * HEAD_DIM:(h + 1) * HEAD_DIM] = (out * (1.0 / total)).astype(obuf.dtype)
            return carry

        lax.fori_loop(0, 2, one_block, 0)

    def out_local(j):
        return pltpu.make_async_copy(
            obuf.at[core, j], o_ref.at[:, cols(core * HALF_KV + j, GROUP * HEAD_DIM)], osem.at[j]
        )

    def out_remote(j, half):
        return pltpu.make_async_remote_copy(
            src_ref=obuf.at[1 - core, j], dst_ref=o_ref.at[:, cols(half * HALF_KV + j, GROUP * HEAD_DIM)],
            send_sem=osend.at[j], recv_sem=orecv.at[j], device_id=partner, device_id_type=MESH,
        )

    for j in range(HALF_KV):
        for part in (0, 1):
            stage(j, part, core).start()
            stage(j, part, 1 - core).start()
        q_stage(j).start()

    barrier = pltpu.get_barrier_semaphore()
    for device in (partner, side_same, side_cross):
        pl.semaphore_signal(barrier, inc=1, device_id=device, device_id_type=MESH)

    @pl.when(has_next)
    def _():
        for device in (next_same, next_cross):
            pl.semaphore_signal(barrier, inc=1, device_id=device, device_id_type=MESH)

    @pl.when(has_prev)
    def _():
        for device in (prev_same, prev_cross):
            pl.semaphore_signal(barrier, inc=1, device_id=device, device_id_type=MESH)

    @pl.when(jnp.logical_not(has_prev))
    def _():
        kv[0:3] = jnp.zeros((3,) + kv.shape[1:], kv.dtype)

        @pl.when(side == 0)
        def _():
            kv[3] = jnp.zeros(kv.shape[1:], kv.dtype)

    pl.semaphore_wait(barrier, 3 + jnp.where(has_next, 2, 0) + jnp.where(has_prev, 2, 0))

    start_direct(0, 0)
    start_direct(0, 1)
    for j in range(HALF_KV):
        q_swap(j, core).start()

    def step(t, carry):
        @pl.when(t < HALF_KV)
        def _():
            exchange(t, 0)
            exchange(t, 1)

        @pl.when(t > 0)
        def _():
            j = t - 1
            await_rest(j)

            @pl.when(has_prev)
            def _():
                attend(j, False)

            @pl.when(jnp.logical_not(has_prev))
            def _():
                attend(j, True)

            out_remote(j, core).start()
            out_local(j).start()

        return carry

    lax.fori_loop(0, HALF_KV + 1, step, 0)

    def finish(j, carry):
        q_swap(j, core).wait_send()
        for part in (0, 1):
            forwards(j, part, lambda copy, slot: None if copy is None else copy.wait_send())
        out_local(j).wait()
        out_remote(j, core).wait_send()
        out_remote(j, 1 - core).wait_recv()
        return carry

    lax.fori_loop(0, HALF_KV, finish, 0)


def fused_body(rows, queries, keys, values):
    tok = queries.shape[0]
    kind = queries.dtype
    wide = GROUP * HEAD_DIM
    dma = pltpu.SemaphoreType.DMA
    return pl.pallas_call(
        functools.partial(fused_kernel, rows),
        out_shape=jax.ShapeDtypeStruct(queries.shape, kind),
        in_specs=[pl.BlockSpec(memory_space=pl.ANY)] * 3,
        out_specs=pl.BlockSpec(memory_space=pl.ANY),
        scratch_shapes=[
            pltpu.VMEM((SLOTS, HALF_KV, 2, tok, HEAD_DIM), kind),
            pltpu.VMEM((HALF_KV, 2, tok, HEAD_DIM), kind),
            pltpu.VMEM((2, HALF_KV, tok, wide), kind),
            pltpu.VMEM((2, HALF_KV, tok, wide), kind),
            dma((HALF_KV, 4)),
            dma((HALF_KV,)),
            dma((HALF_KV,)),
            dma((HALF_KV,)),
            dma((8, HALF_KV, 2)),
            dma((SLOTS, HALF_KV, 2)),
            dma((HALF_KV,)),
            dma((HALF_KV,)),
            dma((HALF_KV,)),
        ],
        compiler_params=pltpu.CompilerParams(
            collective_id=0, has_side_effects=True, vmem_limit_bytes=62 * 1024 * 1024
        ),
        cost_estimate=pl.CostEstimate(
            flops=4 * tok * HEADS * HEAD_DIM * (WINDOW + tok), bytes_accessed=6 * tok * HEADS * HEAD_DIM,
            transcendentals=tok * HEADS * WINDOW,
        ),
        name="window_attention",
    )(queries, keys, values)


def from_behind(x, axis, by):
    peers = lax.axis_size(axis)
    pairs = [(i, i + by) for i in range(peers) if 0 <= i + by < peers]
    return lax.ppermute(x, axis, pairs)


def attend_block(query_rows, key_win, value_win, block_index):
    tok_rows = query_rows.shape[0]
    span_rows = key_win.shape[0]
    row_ids = jnp.arange(tok_rows, dtype=jnp.int32)[:, None]
    col_ids = jnp.arange(span_rows, dtype=jnp.int32)[None, :]
    position = block_index * tok_rows - WINDOW + col_ids
    allowed = (col_ids > row_ids) & (col_ids <= row_ids + WINDOW) & (position >= 0)

    def head_group(head_index):
        query_part = lax.dynamic_slice_in_dim(query_rows, head_index * GROUP * HEAD_DIM, GROUP * HEAD_DIM, 1)
        query_part = query_part.reshape(tok_rows, GROUP, HEAD_DIM)
        key_part = lax.dynamic_slice_in_dim(key_win, head_index * HEAD_DIM, HEAD_DIM, 1)
        value_part = lax.dynamic_slice_in_dim(value_win, head_index * HEAD_DIM, HEAD_DIM, 1)
        score = jnp.einsum(
            "thd,kd->htk", query_part, key_part, preferred_element_type=jnp.float32
        ) * HEAD_DIM ** (-0.5)
        score = jnp.where(allowed[None], score, jnp.float32(-1e30))
        largest = jnp.max(score, axis=2, keepdims=True)
        expo = jnp.where(allowed[None], jnp.exp(score - largest), jnp.float32(0.0))
        total = jnp.sum(expo, axis=2, keepdims=True)
        weight = (expo / total).astype(jnp.bfloat16)
        output = jnp.einsum("htk,kd->thd", weight, value_part, preferred_element_type=jnp.float32)
        return output.astype(jnp.bfloat16).reshape(tok_rows, GROUP * HEAD_DIM)

    parts = lax.map(head_group, jnp.arange(KV_HEADS, dtype=jnp.int32))
    return jnp.transpose(parts, (1, 0, 2)).reshape(tok_rows, HEADS * HEAD_DIM)


def plain_body(queries, keys, values):
    back_blocks = WINDOW // queries.shape[0]
    block_index = lax.axis_index(("blk", "grp"))
    pieces_k = []
    pieces_v = []
    for offset in range(back_blocks, 0, -1):
        moved_k, moved_v = from_behind((keys, values), ("blk", "grp"), offset)
        pieces_k.append(moved_k)
        pieces_v.append(moved_v)
    key_win = jnp.concatenate(pieces_k + [keys], axis=0)
    value_win = jnp.concatenate(pieces_v + [values], axis=0)
    return attend_block(queries, key_win, value_win, block_index)


def solution(mesh):
    blks, grps = mesh.shape["blk"], mesh.shape["grp"]
    placed = P(("blk", "grp"), None)

    def body(queries, keys, values):
        if grps == 2 and blks % 2 == 0 and 4 * queries.shape[0] == WINDOW:
            return fused_body(blks // 2, queries, keys, values)
        return plain_body(queries, keys, values)

    return jax.shard_map(
        body, mesh=mesh, in_specs=(placed, placed, placed), out_specs=placed, check_vma=False
    )
```

```python
import functools

import jax
import jax.numpy as jnp
from jax import lax
from jax.experimental import pallas as pl
from jax.experimental.pallas import tpu as pltpu
from jax.sharding import PartitionSpec as P

HEADS = 16
KV_HEADS = 8
HEAD_DIM = 128
WINDOW = 1024
GROUP = HEADS // KV_HEADS
HALF_KV = KV_HEADS // 2
SLOTS = 7
SCALE_LOG2E = HEAD_DIM ** -0.5 * 1.4426950408889634
MESH = pl.DeviceIdType.MESH


def fused_kernel(
    rows, q_ref, k_ref, v_ref, o_ref, kv, other, qbuf, wbuf, obuf,
    stage_sem, qstage_sem, qsend, qrecv, send, recv, osem, osend, orecv,
):
    blk = lax.axis_index("blk")
    side = lax.axis_index("grp")
    row = blk // 2
    core = blk % 2
    tok = q_ref.shape[0]
    has_prev = row > 0
    has_next = row < rows - 1
    own_slot = 4 + 2 * core

    partner = (2 * row + 1 - core, side)
    next_same = (2 * row + 2 + core, side)
    next_cross = (2 * row + 3 - core, side)
    side_same = (2 * row + core, 1 - side)
    side_cross = (2 * row + 1 - core, 1 - side)
    prev_same = (2 * row - 2 + core, side)
    prev_cross = (2 * row - 1 - core, side)

    def cols(index, width):
        return pl.ds(pl.multiple_of(index * width, width), width)

    def stage(j, part, half):
        source = (k_ref, v_ref)[part].at[:, cols(half * HALF_KV + j, HEAD_DIM)]
        if half is core:
            return pltpu.make_async_copy(source, kv.at[own_slot, j, part], stage_sem.at[j, 2 + part])
        return pltpu.make_async_copy(source, other.at[j, part], stage_sem.at[j, part])

    def q_stage(j):
        mine = cols(core * HALF_KV + j, GROUP * HEAD_DIM)
        return pltpu.make_async_copy(q_ref.at[:, mine], qbuf.at[core, j], qstage_sem.at[j])

    def q_swap(j, block):
        rest = cols((1 - core) * HALF_KV + j, GROUP * HEAD_DIM)
        return pltpu.make_async_remote_copy(
            src_ref=q_ref.at[:, rest], dst_ref=qbuf.at[block, j],
            send_sem=qsend.at[j], recv_sem=qrecv.at[j], device_id=partner, device_id_type=MESH,
        )

    def remote(src, dst, kind, arrival, j, part, device):
        return pltpu.make_async_remote_copy(
            src_ref=src, dst_ref=dst, send_sem=send.at[kind, j, part], recv_sem=recv.at[arrival, j, part],
            device_id=device, device_id_type=MESH,
        )

    def piece(slot, j, part):
        return kv.at[slot, j, part]

    def to_partner(j, part):
        return remote(other.at[j, part], piece(own_slot, j, part), 0, own_slot, j, part, partner)

    def to_next(j, part):
        slot = 2 * core
        return [
            remote(piece(own_slot, j, part), piece(slot, j, part), 1, slot, j, part, next_same),
            remote(other.at[j, part], piece(slot, j, part), 2, slot, j, part, next_cross),
        ]

    def to_side(j, part):
        slot = jnp.where(side == 0, 3 + 2 * core, 5)
        return [
            remote(piece(own_slot, j, part), piece(slot, j, part), 3, slot, j, part, side_same),
            remote(other.at[j, part], piece(slot, j, part), 4, slot, j, part, side_cross),
        ]

    sends_side = jnp.logical_or(side == 0, core == 0)

    def pass_side(j, part, slot, to_slot, kind):
        return remote(piece(slot, j, part), piece(to_slot, j, part), kind, to_slot, j, part, side_same)

    def pass_next(j):
        return remote(piece(5, j, 1), piece(1, j, 1), 6, 1, j, 1, next_same)

    def arrived(slot, j, part):
        remote(piece(slot, j, part), piece(slot, j, part), 0, slot, j, part, partner).wait_recv()

    def direct_side(j, part, act):
        @pl.when(sends_side)
        def _():
            for copy in to_side(j, part):
                act(copy)

    def direct_next(j, part, act):
        act(to_partner(j, part))

        @pl.when(has_next)
        def _():
            for copy in to_next(j, part):
                act(copy)

    def forwards(j, part, act):
        @pl.when(jnp.logical_and(has_prev, side == 1))
        def _():
            act(pass_side(j, part, 2, 3, 5), 2)
            if part == 0:
                act(pass_side(j, part, 0, 1, 7), 0)
            else:
                act(None, 0)

        @pl.when(jnp.logical_and(has_prev, side == 0))
        def _():
            act(pass_side(j, part, 2, 1, 5) if part == 0 else None, 2)
            act(None, 0)

        if part == 0:
            act(None, 5)
        else:
            @pl.when(has_next)
            def _():
                act(pass_next(j), 5)

            @pl.when(jnp.logical_not(has_next))
            def _():
                act(None, 5)

    def launch(copy):
        copy.start()

    def sent(copy):
        copy.wait_send()

    def start_direct(j, part):
        stage(j, part, core).wait()
        stage(j, part, 1 - core).wait()
        direct_side(j, part, launch)
        direct_next(j, part, launch)

    def exchange(j, part):
        def hand_on(copy, slot):
            arrived(slot, j, part)
            if copy is not None:
                copy.start()

        forwards(j, part, hand_on)
        direct_side(j, part, sent)
        direct_next(j, part, sent)

        @pl.when(j < HALF_KV - 1 - part)
        def _():
            start_direct(j + 1 + part, 1 - part)

    def arrived_rest(j, part):
        arrived(6 - 2 * core, j, part)

        @pl.when(jnp.logical_or(side == 1, has_prev))
        def _():
            arrived(3, j, part)

        @pl.when(has_prev)
        def _():
            arrived(1, j, part)

    def weigh_chunk(j):
        q_stage(j).wait()
        q_swap(j, 1 - core).wait_recv()
        arrived_rest(j, 0)

        @pl.when(has_prev)
        def _():
            weigh(j, False)

        @pl.when(jnp.logical_not(has_prev))
        def _():
            weigh(j, True)

    def blend_chunk(j):
        arrived_rest(j, 1)
        blend(j, 1 - core)
        out_remote(j, core).start()
        blend(j, core)
        out_local(j).start()

    def weigh(j, masked):
        upper = (
            lax.broadcasted_iota(jnp.int32, (tok, tok), 1) > lax.broadcasted_iota(jnp.int32, (tok, tok), 0)
        )

        def one_block(block, carry):
            base = 2 * block
            for h in range(GROUP):
                q = qbuf[block, j, :, h * HEAD_DIM:(h + 1) * HEAD_DIM]
                score = []
                for i in range(5):
                    s = lax.dot_general(
                        q, kv[base + i, j, 0], (((1,), (1,)), ((), ())), preferred_element_type=jnp.float32
                    )
                    if masked and i < 4:
                        s = jnp.where(4 * row + side + base + i >= 4, s, jnp.float32(-1e30))
                    score.append(s)
                score = [jnp.where(upper, score[0], score[4])] + score[1:4]
                top = jnp.max(jnp.maximum(jnp.maximum(score[0], score[1]), jnp.maximum(score[2], score[3])),
                              axis=1, keepdims=True)
                expo = [jnp.exp2((s - top) * jnp.float32(SCALE_LOG2E)) for s in score]
                total = jnp.sum((expo[0] + expo[1]) + (expo[2] + expo[3]), axis=1, keepdims=True)
                share = 1.0 / total
                expo = [e * share for e in expo]
                zero = jnp.zeros_like(expo[0])
                weight = [jnp.where(upper, expo[0], zero)] + expo[1:] + [jnp.where(upper, zero, expo[0])]
                for i in range(5):
                    wbuf[block, i, h * tok:(h + 1) * tok, :] = weight[i].astype(wbuf.dtype)
            return carry

        lax.fori_loop(0, 2, one_block, 0)

    def blend(j, block):
        base = 2 * block
        out = None
        for i in range(5):
            term = jnp.dot(wbuf[block, i], kv[base + i, j, 1], preferred_element_type=jnp.float32)
            out = term if out is None else out + term
        out = out.astype(obuf.dtype)
        for h in range(GROUP):
            obuf[block, j, :, h * HEAD_DIM:(h + 1) * HEAD_DIM] = out[h * tok:(h + 1) * tok]

    def out_local(j):
        return pltpu.make_async_copy(
            obuf.at[core, j], o_ref.at[:, cols(core * HALF_KV + j, GROUP * HEAD_DIM)], osem.at[j]
        )

    def out_remote(j, half):
        return pltpu.make_async_remote_copy(
            src_ref=obuf.at[1 - core, j], dst_ref=o_ref.at[:, cols(half * HALF_KV + j, GROUP * HEAD_DIM)],
            send_sem=osend.at[j], recv_sem=orecv.at[j], device_id=partner, device_id_type=MESH,
        )

    for j in range(HALF_KV):
        for part in (0, 1):
            stage(j, part, core).start()
            stage(j, part, 1 - core).start()
        q_stage(j).start()

    barrier = pltpu.get_barrier_semaphore()
    for device in (partner, side_same, side_cross):
        pl.semaphore_signal(barrier, inc=1, device_id=device, device_id_type=MESH)

    @pl.when(has_next)
    def _():
        for device in (next_same, next_cross):
            pl.semaphore_signal(barrier, inc=1, device_id=device, device_id_type=MESH)

    @pl.when(has_prev)
    def _():
        for device in (prev_same, prev_cross):
            pl.semaphore_signal(barrier, inc=1, device_id=device, device_id_type=MESH)

    @pl.when(jnp.logical_not(has_prev))
    def _():
        kv[0:3] = jnp.zeros((3,) + kv.shape[1:], kv.dtype)

        @pl.when(side == 0)
        def _():
            kv[3] = jnp.zeros(kv.shape[1:], kv.dtype)

    pl.semaphore_wait(barrier, 3 + jnp.where(has_next, 2, 0) + jnp.where(has_prev, 2, 0))

    start_direct(0, 0)
    for j in range(HALF_KV):
        q_swap(j, core).start()
    start_direct(0, 1)
    start_direct(1, 0)

    def step(j, carry):
        @pl.when(j < HALF_KV)
        def _():
            exchange(j, 0)

        @pl.when(j > 0)
        def _():
            blend_chunk(j - 1)

        @pl.when(j < HALF_KV)
        def _():
            exchange(j, 1)
            weigh_chunk(j)

        return carry

    lax.fori_loop(0, HALF_KV + 1, step, 0)

    def finish(j, carry):
        q_swap(j, core).wait_send()
        for part in (0, 1):
            forwards(j, part, lambda copy, slot: None if copy is None else copy.wait_send())
        out_local(j).wait()
        out_remote(j, core).wait_send()
        out_remote(j, 1 - core).wait_recv()
        return carry

    lax.fori_loop(0, HALF_KV, finish, 0)


def fused_body(rows, queries, keys, values):
    tok = queries.shape[0]
    kind = queries.dtype
    wide = GROUP * HEAD_DIM
    dma = pltpu.SemaphoreType.DMA
    return pl.pallas_call(
        functools.partial(fused_kernel, rows),
        out_shape=jax.ShapeDtypeStruct(queries.shape, kind),
        in_specs=[pl.BlockSpec(memory_space=pl.ANY)] * 3,
        out_specs=pl.BlockSpec(memory_space=pl.ANY),
        scratch_shapes=[
            pltpu.VMEM((SLOTS, HALF_KV, 2, tok, HEAD_DIM), kind),
            pltpu.VMEM((HALF_KV, 2, tok, HEAD_DIM), kind),
            pltpu.VMEM((2, HALF_KV, tok, wide), kind),
            pltpu.VMEM((2, 5, GROUP * tok, tok), kind),
            pltpu.VMEM((2, HALF_KV, tok, wide), kind),
            dma((HALF_KV, 4)),
            dma((HALF_KV,)),
            dma((HALF_KV,)),
            dma((HALF_KV,)),
            dma((8, HALF_KV, 2)),
            dma((SLOTS, HALF_KV, 2)),
            dma((HALF_KV,)),
            dma((HALF_KV,)),
            dma((HALF_KV,)),
        ],
        compiler_params=pltpu.CompilerParams(
            collective_id=0, has_side_effects=True, vmem_limit_bytes=58 * 1024 * 1024
        ),
        cost_estimate=pl.CostEstimate(
            flops=4 * tok * HEADS * HEAD_DIM * (WINDOW + tok), bytes_accessed=6 * tok * HEADS * HEAD_DIM,
            transcendentals=tok * HEADS * WINDOW,
        ),
        name="window_attention",
    )(queries, keys, values)


def from_behind(x, axis, by):
    peers = lax.axis_size(axis)
    pairs = [(i, i + by) for i in range(peers) if 0 <= i + by < peers]
    return lax.ppermute(x, axis, pairs)


def attend_block(query_rows, key_win, value_win, block_index):
    tok_rows = query_rows.shape[0]
    span_rows = key_win.shape[0]
    row_ids = jnp.arange(tok_rows, dtype=jnp.int32)[:, None]
    col_ids = jnp.arange(span_rows, dtype=jnp.int32)[None, :]
    position = block_index * tok_rows - WINDOW + col_ids
    allowed = (col_ids > row_ids) & (col_ids <= row_ids + WINDOW) & (position >= 0)

    def head_group(head_index):
        query_part = lax.dynamic_slice_in_dim(query_rows, head_index * GROUP * HEAD_DIM, GROUP * HEAD_DIM, 1)
        query_part = query_part.reshape(tok_rows, GROUP, HEAD_DIM)
        key_part = lax.dynamic_slice_in_dim(key_win, head_index * HEAD_DIM, HEAD_DIM, 1)
        value_part = lax.dynamic_slice_in_dim(value_win, head_index * HEAD_DIM, HEAD_DIM, 1)
        score = jnp.einsum(
            "thd,kd->htk", query_part, key_part, preferred_element_type=jnp.float32
        ) * HEAD_DIM ** (-0.5)
        score = jnp.where(allowed[None], score, jnp.float32(-1e30))
        largest = jnp.max(score, axis=2, keepdims=True)
        expo = jnp.where(allowed[None], jnp.exp(score - largest), jnp.float32(0.0))
        total = jnp.sum(expo, axis=2, keepdims=True)
        weight = (expo / total).astype(jnp.bfloat16)
        output = jnp.einsum("htk,kd->thd", weight, value_part, preferred_element_type=jnp.float32)
        return output.astype(jnp.bfloat16).reshape(tok_rows, GROUP * HEAD_DIM)

    parts = lax.map(head_group, jnp.arange(KV_HEADS, dtype=jnp.int32))
    return jnp.transpose(parts, (1, 0, 2)).reshape(tok_rows, HEADS * HEAD_DIM)


def plain_body(queries, keys, values):
    back_blocks = WINDOW // queries.shape[0]
    block_index = lax.axis_index(("blk", "grp"))
    pieces_k = []
    pieces_v = []
    for offset in range(back_blocks, 0, -1):
        moved_k, moved_v = from_behind((keys, values), ("blk", "grp"), offset)
        pieces_k.append(moved_k)
        pieces_v.append(moved_v)
    key_win = jnp.concatenate(pieces_k + [keys], axis=0)
    value_win = jnp.concatenate(pieces_v + [values], axis=0)
    return attend_block(queries, key_win, value_win, block_index)


def solution(mesh):
    blks, grps = mesh.shape["blk"], mesh.shape["grp"]
    placed = P(("blk", "grp"), None)

    def body(queries, keys, values):
        if grps == 2 and blks % 2 == 0 and 4 * queries.shape[0] == WINDOW:
            return fused_body(blks // 2, queries, keys, values)
        return plain_body(queries, keys, values)

    return jax.shard_map(
        body, mesh=mesh, in_specs=(placed, placed, placed), out_specs=placed, check_vma=False
    )
```

```python
import functools

import jax
import jax.numpy as jnp
from jax import lax
from jax.experimental import pallas as pl
from jax.experimental.pallas import tpu as pltpu
from jax.sharding import PartitionSpec as P

HEADS = 16
KV_HEADS = 8
HEAD_DIM = 128
WINDOW = 1024
GROUP = HEADS // KV_HEADS
HALF_KV = KV_HEADS // 2
SLOTS = 7
SCALE_LOG2E = HEAD_DIM ** -0.5 * 1.4426950408889634
MESH = pl.DeviceIdType.MESH


def fused_kernel(
    rows, q_ref, k_ref, v_ref, o_ref, kv, other, qbuf, wbuf, obuf,
    stage_sem, qstage_sem, qsend, qrecv, send, recv, osem, osend, orecv,
):
    blk = lax.axis_index("blk")
    side = lax.axis_index("grp")
    row = blk // 2
    core = blk % 2
    tok = q_ref.shape[0]
    has_prev = row > 0
    has_next = row < rows - 1
    own_slot = 4 + 2 * core

    partner = (2 * row + 1 - core, side)
    next_same = (2 * row + 2 + core, side)
    next_cross = (2 * row + 3 - core, side)
    side_same = (2 * row + core, 1 - side)
    side_cross = (2 * row + 1 - core, 1 - side)
    prev_same = (2 * row - 2 + core, side)
    prev_cross = (2 * row - 1 - core, side)

    def cols(index, width):
        return pl.ds(pl.multiple_of(index * width, width), width)

    def stage(j, part, half):
        source = (k_ref, v_ref)[part].at[:, cols(half * HALF_KV + j, HEAD_DIM)]
        if half is core:
            return pltpu.make_async_copy(source, kv.at[own_slot, j, part], stage_sem.at[j, 2 + part])
        return pltpu.make_async_copy(source, other.at[j, part], stage_sem.at[j, part])

    def q_stage(j):
        mine = cols(core * HALF_KV + j, GROUP * HEAD_DIM)
        return pltpu.make_async_copy(q_ref.at[:, mine], qbuf.at[core, j], qstage_sem.at[j])

    def q_swap(j, block):
        rest = cols((1 - core) * HALF_KV + j, GROUP * HEAD_DIM)
        return pltpu.make_async_remote_copy(
            src_ref=q_ref.at[:, rest], dst_ref=qbuf.at[block, j],
            send_sem=qsend.at[j], recv_sem=qrecv.at[j], device_id=partner, device_id_type=MESH,
        )

    def remote(src, dst, kind, arrival, j, part, device):
        return pltpu.make_async_remote_copy(
            src_ref=src, dst_ref=dst, send_sem=send.at[kind, j, part], recv_sem=recv.at[arrival, j, part],
            device_id=device, device_id_type=MESH,
        )

    def piece(slot, j, part):
        return kv.at[slot, j, part]

    def to_partner(j, part):
        return remote(other.at[j, part], piece(own_slot, j, part), 0, own_slot, j, part, partner)

    def to_next(j, part):
        slot = 2 * core
        return [
            remote(piece(own_slot, j, part), piece(slot, j, part), 1, slot, j, part, next_same),
            remote(other.at[j, part], piece(slot, j, part), 2, slot, j, part, next_cross),
        ]

    def to_side(j, part):
        slot = jnp.where(side == 0, 3 + 2 * core, 5)
        return [
            remote(piece(own_slot, j, part), piece(slot, j, part), 3, slot, j, part, side_same),
            remote(other.at[j, part], piece(slot, j, part), 4, slot, j, part, side_cross),
        ]

    sends_side = jnp.logical_or(side == 0, core == 0)

    def pass_side(j, part, slot, to_slot, kind):
        return remote(piece(slot, j, part), piece(to_slot, j, part), kind, to_slot, j, part, side_same)

    def pass_next(j):
        return remote(piece(5, j, 1), piece(1, j, 1), 6, 1, j, 1, next_same)

    def arrived(slot, j, part):
        remote(piece(slot, j, part), piece(slot, j, part), 0, slot, j, part, partner).wait_recv()

    def direct_side(j, part, act):
        @pl.when(sends_side)
        def _():
            for copy in to_side(j, part):
                act(copy)

    def direct_next(j, part, act):
        act(to_partner(j, part))

        @pl.when(has_next)
        def _():
            for copy in to_next(j, part):
                act(copy)

    def forwards(j, part, act):
        @pl.when(jnp.logical_and(has_prev, side == 1))
        def _():
            act(pass_side(j, part, 2, 3, 5), 2)
            if part == 0:
                act(pass_side(j, part, 0, 1, 7), 0)
            else:
                act(None, 0)

        @pl.when(jnp.logical_and(has_prev, side == 0))
        def _():
            act(pass_side(j, part, 2, 1, 5) if part == 0 else None, 2)
            act(None, 0)

        if part == 0:
            act(None, 5)
        else:
            @pl.when(has_next)
            def _():
                act(pass_next(j), 5)

            @pl.when(jnp.logical_not(has_next))
            def _():
                act(None, 5)

    def launch(copy):
        copy.start()

    def sent(copy):
        copy.wait_send()

    def staged(j, part):
        stage(j, part, core).wait()
        stage(j, part, 1 - core).wait()

    def exchange(j, part):
        def hand_on(copy, slot):
            arrived(slot, j, part)
            if copy is not None:
                copy.start()

        forwards(j, part, hand_on)
        direct_side(j, part, sent)
        direct_next(j, part, sent)

        @pl.when(j < HALF_KV - 1 - part)
        def _():
            direct_next(j + 1 + part, 1 - part, launch)

        @pl.when(jnp.logical_and(side == 0, j < HALF_KV - 1 - part))
        def _():
            direct_side(j + 1 + part, 1 - part, launch)

        @pl.when(jnp.logical_and(side == 1, j < HALF_KV - 2 - part))
        def _():
            direct_side(j + 2 + part, 1 - part, launch)

    def arrived_rest(j, part):
        arrived(6 - 2 * core, j, part)

        @pl.when(jnp.logical_or(side == 1, has_prev))
        def _():
            arrived(3, j, part)

        @pl.when(has_prev)
        def _():
            arrived(1, j, part)

    def weigh_chunk(j):
        q_stage(j).wait()
        q_swap(j, 1 - core).wait_recv()
        arrived_rest(j, 0)

        @pl.when(has_prev)
        def _():
            weigh(j, False)

        @pl.when(jnp.logical_not(has_prev))
        def _():
            weigh(j, True)

    def blend_chunk(j):
        arrived_rest(j, 1)
        blend(j, 1 - core)
        out_remote(j, core).start()
        blend(j, core)
        out_local(j).start()

    def weigh(j, masked):
        upper = (
            lax.broadcasted_iota(jnp.int32, (tok, tok), 1) > lax.broadcasted_iota(jnp.int32, (tok, tok), 0)
        )

        def one_block(block, carry):
            base = 2 * block
            for h in range(GROUP):
                q = qbuf[block, j, :, h * HEAD_DIM:(h + 1) * HEAD_DIM]
                score = []
                for i in range(5):
                    s = lax.dot_general(
                        q, kv[base + i, j, 0], (((1,), (1,)), ((), ())), preferred_element_type=jnp.float32
                    )
                    if masked and i < 4:
                        s = jnp.where(4 * row + side + base + i >= 4, s, jnp.float32(-1e30))
                    score.append(s)
                score = [jnp.where(upper, score[0], score[4])] + score[1:4]
                top = jnp.max(jnp.maximum(jnp.maximum(score[0], score[1]), jnp.maximum(score[2], score[3])),
                              axis=1, keepdims=True)
                expo = [jnp.exp2((s - top) * jnp.float32(SCALE_LOG2E)) for s in score]
                total = jnp.sum((expo[0] + expo[1]) + (expo[2] + expo[3]), axis=1, keepdims=True)
                share = 1.0 / total
                expo = [e * share for e in expo]
                zero = jnp.zeros_like(expo[0])
                weight = [jnp.where(upper, expo[0], zero)] + expo[1:] + [jnp.where(upper, zero, expo[0])]
                for i in range(5):
                    wbuf[block, i, h * tok:(h + 1) * tok, :] = weight[i].astype(wbuf.dtype)
            return carry

        lax.fori_loop(0, 2, one_block, 0)

    def blend(j, block):
        base = 2 * block
        out = None
        for i in range(5):
            term = jnp.dot(wbuf[block, i], kv[base + i, j, 1], preferred_element_type=jnp.float32)
            out = term if out is None else out + term
        out = out.astype(obuf.dtype)
        for h in range(GROUP):
            obuf[block, j, :, h * HEAD_DIM:(h + 1) * HEAD_DIM] = out[h * tok:(h + 1) * tok]

    def out_local(j):
        return pltpu.make_async_copy(
            obuf.at[core, j], o_ref.at[:, cols(core * HALF_KV + j, GROUP * HEAD_DIM)], osem.at[j]
        )

    def out_remote(j, half):
        return pltpu.make_async_remote_copy(
            src_ref=obuf.at[1 - core, j], dst_ref=o_ref.at[:, cols(half * HALF_KV + j, GROUP * HEAD_DIM)],
            send_sem=osend.at[j], recv_sem=orecv.at[j], device_id=partner, device_id_type=MESH,
        )

    for j in range(HALF_KV):
        for part in (0, 1):
            stage(j, part, core).start()
            stage(j, part, 1 - core).start()
        q_stage(j).start()

    barrier = pltpu.get_barrier_semaphore()
    for device in (partner, side_same, side_cross):
        pl.semaphore_signal(barrier, inc=1, device_id=device, device_id_type=MESH)

    @pl.when(has_next)
    def _():
        for device in (next_same, next_cross):
            pl.semaphore_signal(barrier, inc=1, device_id=device, device_id_type=MESH)

    @pl.when(has_prev)
    def _():
        for device in (prev_same, prev_cross):
            pl.semaphore_signal(barrier, inc=1, device_id=device, device_id_type=MESH)

    @pl.when(jnp.logical_not(has_prev))
    def _():
        kv[0:3] = jnp.zeros((3,) + kv.shape[1:], kv.dtype)

        @pl.when(side == 0)
        def _():
            kv[3] = jnp.zeros(kv.shape[1:], kv.dtype)

    pl.semaphore_wait(barrier, 3 + jnp.where(has_next, 2, 0) + jnp.where(has_prev, 2, 0))

    for j, part in ((0, 0), (0, 1), (1, 0)):
        staged(j, part)
        direct_next(j, part, launch)
        direct_side(j, part, launch)
        if part == 0:
            q_swap(j, core).start()
    for j, part in ((1, 1), (2, 0), (2, 1), (3, 0), (3, 1)):
        staged(j, part)
        if part == 0:
            q_swap(j, core).start()

    @pl.when(side == 1)
    def _():
        direct_side(1, 1, launch)
        direct_side(2, 0, launch)

    def step(j, carry):
        @pl.when(j < HALF_KV)
        def _():
            exchange(j, 0)

        @pl.when(j > 0)
        def _():
            weigh_chunk(j - 1)

        @pl.when(j < HALF_KV)
        def _():
            exchange(j, 1)

        @pl.when(j > 0)
        def _():
            blend_chunk(j - 1)

        return carry

    lax.fori_loop(0, HALF_KV + 1, step, 0)

    def finish(j, carry):
        q_swap(j, core).wait_send()
        for part in (0, 1):
            forwards(j, part, lambda copy, slot: None if copy is None else copy.wait_send())
        out_local(j).wait()
        out_remote(j, core).wait_send()
        out_remote(j, 1 - core).wait_recv()
        return carry

    lax.fori_loop(0, HALF_KV, finish, 0)


def fused_body(rows, queries, keys, values):
    tok = queries.shape[0]
    kind = queries.dtype
    wide = GROUP * HEAD_DIM
    dma = pltpu.SemaphoreType.DMA
    return pl.pallas_call(
        functools.partial(fused_kernel, rows),
        out_shape=jax.ShapeDtypeStruct(queries.shape, kind),
        in_specs=[pl.BlockSpec(memory_space=pl.ANY)] * 3,
        out_specs=pl.BlockSpec(memory_space=pl.ANY),
        scratch_shapes=[
            pltpu.VMEM((SLOTS, HALF_KV, 2, tok, HEAD_DIM), kind),
            pltpu.VMEM((HALF_KV, 2, tok, HEAD_DIM), kind),
            pltpu.VMEM((2, HALF_KV, tok, wide), kind),
            pltpu.VMEM((2, 5, GROUP * tok, tok), kind),
            pltpu.VMEM((2, HALF_KV, tok, wide), kind),
            dma((HALF_KV, 4)),
            dma((HALF_KV,)),
            dma((HALF_KV,)),
            dma((HALF_KV,)),
            dma((8, HALF_KV, 2)),
            dma((SLOTS, HALF_KV, 2)),
            dma((HALF_KV,)),
            dma((HALF_KV,)),
            dma((HALF_KV,)),
        ],
        compiler_params=pltpu.CompilerParams(
            collective_id=0, has_side_effects=True, vmem_limit_bytes=58 * 1024 * 1024
        ),
        cost_estimate=pl.CostEstimate(
            flops=4 * tok * HEADS * HEAD_DIM * (WINDOW + tok), bytes_accessed=6 * tok * HEADS * HEAD_DIM,
            transcendentals=tok * HEADS * WINDOW,
        ),
        name="window_attention",
    )(queries, keys, values)


def from_behind(x, axis, by):
    peers = lax.axis_size(axis)
    pairs = [(i, i + by) for i in range(peers) if 0 <= i + by < peers]
    return lax.ppermute(x, axis, pairs)


def attend_block(query_rows, key_win, value_win, block_index):
    tok_rows = query_rows.shape[0]
    span_rows = key_win.shape[0]
    row_ids = jnp.arange(tok_rows, dtype=jnp.int32)[:, None]
    col_ids = jnp.arange(span_rows, dtype=jnp.int32)[None, :]
    position = block_index * tok_rows - WINDOW + col_ids
    allowed = (col_ids > row_ids) & (col_ids <= row_ids + WINDOW) & (position >= 0)

    def head_group(head_index):
        query_part = lax.dynamic_slice_in_dim(query_rows, head_index * GROUP * HEAD_DIM, GROUP * HEAD_DIM, 1)
        query_part = query_part.reshape(tok_rows, GROUP, HEAD_DIM)
        key_part = lax.dynamic_slice_in_dim(key_win, head_index * HEAD_DIM, HEAD_DIM, 1)
        value_part = lax.dynamic_slice_in_dim(value_win, head_index * HEAD_DIM, HEAD_DIM, 1)
        score = jnp.einsum(
            "thd,kd->htk", query_part, key_part, preferred_element_type=jnp.float32
        ) * HEAD_DIM ** (-0.5)
        score = jnp.where(allowed[None], score, jnp.float32(-1e30))
        largest = jnp.max(score, axis=2, keepdims=True)
        expo = jnp.where(allowed[None], jnp.exp(score - largest), jnp.float32(0.0))
        total = jnp.sum(expo, axis=2, keepdims=True)
        weight = (expo / total).astype(jnp.bfloat16)
        output = jnp.einsum("htk,kd->thd", weight, value_part, preferred_element_type=jnp.float32)
        return output.astype(jnp.bfloat16).reshape(tok_rows, GROUP * HEAD_DIM)

    parts = lax.map(head_group, jnp.arange(KV_HEADS, dtype=jnp.int32))
    return jnp.transpose(parts, (1, 0, 2)).reshape(tok_rows, HEADS * HEAD_DIM)


def plain_body(queries, keys, values):
    back_blocks = WINDOW // queries.shape[0]
    block_index = lax.axis_index(("blk", "grp"))
    pieces_k = []
    pieces_v = []
    for offset in range(back_blocks, 0, -1):
        moved_k, moved_v = from_behind((keys, values), ("blk", "grp"), offset)
        pieces_k.append(moved_k)
        pieces_v.append(moved_v)
    key_win = jnp.concatenate(pieces_k + [keys], axis=0)
    value_win = jnp.concatenate(pieces_v + [values], axis=0)
    return attend_block(queries, key_win, value_win, block_index)


def solution(mesh):
    blks, grps = mesh.shape["blk"], mesh.shape["grp"]
    placed = P(("blk", "grp"), None)

    def body(queries, keys, values):
        if grps == 2 and blks % 2 == 0 and 4 * queries.shape[0] == WINDOW:
            return fused_body(blks // 2, queries, keys, values)
        return plain_body(queries, keys, values)

    return jax.shard_map(
        body, mesh=mesh, in_specs=(placed, placed, placed), out_specs=placed, check_vma=False
    )
```

```python
import functools

import jax
import jax.numpy as jnp
from jax import lax
from jax.experimental import pallas as pl
from jax.experimental.pallas import tpu as pltpu
from jax.sharding import PartitionSpec as P

HEADS = 16
KV_HEADS = 8
HEAD_DIM = 128
WINDOW = 1024
GROUP = HEADS // KV_HEADS
HALF_KV = KV_HEADS // 2
SLOTS = 7
TILE = 16
SCALE_LOG2E = HEAD_DIM ** -0.5 * 1.4426950408889634
MESH = pl.DeviceIdType.MESH


def fused_kernel(
    rows, q_ref, k_ref, v_ref, o_ref, kv, other, qbuf, sbuf, wbuf, obuf,
    stage_sem, qstage_sem, qsend, qrecv, send, recv, osem, osend, orecv,
):
    blk = lax.axis_index("blk")
    side = lax.axis_index("grp")
    row = blk // 2
    core = blk % 2
    tok = q_ref.shape[0]
    has_prev = row > 0
    has_next = row < rows - 1
    own_slot = 4 + 2 * core

    partner = (2 * row + 1 - core, side)
    next_same = (2 * row + 2 + core, side)
    next_cross = (2 * row + 3 - core, side)
    side_same = (2 * row + core, 1 - side)
    side_cross = (2 * row + 1 - core, 1 - side)
    prev_same = (2 * row - 2 + core, side)
    prev_cross = (2 * row - 1 - core, side)

    def cols(index, width):
        return pl.ds(pl.multiple_of(index * width, width), width)

    def stage(j, part, half):
        source = (k_ref, v_ref)[part].at[:, cols(half * HALF_KV + j, HEAD_DIM)]
        if half is core:
            return pltpu.make_async_copy(source, kv.at[own_slot, j, part], stage_sem.at[j, 2 + part])
        return pltpu.make_async_copy(source, other.at[j, part], stage_sem.at[j, part])

    def q_stage(j):
        mine = cols(core * HALF_KV + j, GROUP * HEAD_DIM)
        return pltpu.make_async_copy(q_ref.at[:, mine], qbuf.at[core, j], qstage_sem.at[j])

    def q_swap(j, block):
        rest = cols((1 - core) * HALF_KV + j, GROUP * HEAD_DIM)
        return pltpu.make_async_remote_copy(
            src_ref=q_ref.at[:, rest], dst_ref=qbuf.at[block, j],
            send_sem=qsend.at[j], recv_sem=qrecv.at[j], device_id=partner, device_id_type=MESH,
        )

    def remote(src, dst, kind, arrival, j, part, device):
        return pltpu.make_async_remote_copy(
            src_ref=src, dst_ref=dst, send_sem=send.at[kind, j, part], recv_sem=recv.at[arrival, j, part],
            device_id=device, device_id_type=MESH,
        )

    def piece(slot, j, part):
        return kv.at[slot, j, part]

    def to_partner(j, part):
        return remote(other.at[j, part], piece(own_slot, j, part), 0, own_slot, j, part, partner)

    def to_next(j, part):
        slot = 2 * core
        return [
            remote(piece(own_slot, j, part), piece(slot, j, part), 1, slot, j, part, next_same),
            remote(other.at[j, part], piece(slot, j, part), 2, slot, j, part, next_cross),
        ]

    def to_side(j, part):
        slot = jnp.where(side == 0, 3 + 2 * core, 5)
        return [
            remote(piece(own_slot, j, part), piece(slot, j, part), 3, slot, j, part, side_same),
            remote(other.at[j, part], piece(slot, j, part), 4, slot, j, part, side_cross),
        ]

    sends_side = jnp.logical_or(side == 0, core == 0)

    def pass_side(j, part, slot, to_slot, kind):
        return remote(piece(slot, j, part), piece(to_slot, j, part), kind, to_slot, j, part, side_same)

    def pass_next(j):
        return remote(piece(5, j, 1), piece(1, j, 1), 6, 1, j, 1, next_same)

    def arrived(slot, j, part):
        remote(piece(slot, j, part), piece(slot, j, part), 0, slot, j, part, partner).wait_recv()

    def direct_side(j, part, act):
        @pl.when(sends_side)
        def _():
            for copy in to_side(j, part):
                act(copy)

    def direct_next(j, part, act):
        act(to_partner(j, part))

        @pl.when(has_next)
        def _():
            for copy in to_next(j, part):
                act(copy)

    def forwards(j, part, act):
        @pl.when(jnp.logical_and(has_prev, side == 1))
        def _():
            act(pass_side(j, part, 2, 3, 5), 2)
            if part == 0:
                act(pass_side(j, part, 0, 1, 7), 0)
            else:
                act(None, 0)

        @pl.when(jnp.logical_and(has_prev, side == 0))
        def _():
            act(pass_side(j, part, 2, 1, 5) if part == 0 else None, 2)
            act(None, 0)

        if part == 0:
            act(None, 5)
        else:
            @pl.when(has_next)
            def _():
                act(pass_next(j), 5)

            @pl.when(jnp.logical_not(has_next))
            def _():
                act(None, 5)

    def launch(copy):
        copy.start()

    def sent(copy):
        copy.wait_send()

    def staged(j, part):
        stage(j, part, core).wait()
        stage(j, part, 1 - core).wait()

    def exchange(j, part):
        def hand_on(copy, slot):
            arrived(slot, j, part)
            if copy is not None:
                copy.start()

        forwards(j, part, hand_on)
        direct_side(j, part, sent)
        direct_next(j, part, sent)

        @pl.when(j < HALF_KV - 1 - part)
        def _():
            direct_next(j + 1 + part, 1 - part, launch)

        @pl.when(jnp.logical_and(side == 0, j < HALF_KV - 1 - part))
        def _():
            direct_side(j + 1 + part, 1 - part, launch)

        @pl.when(jnp.logical_and(side == 1, j < HALF_KV - 2 - part))
        def _():
            direct_side(j + 2 + part, 1 - part, launch)

    def arrived_rest(j, part):
        arrived(6 - 2 * core, j, part)

        @pl.when(jnp.logical_or(side == 1, has_prev))
        def _():
            arrived(3, j, part)

        @pl.when(has_prev)
        def _():
            arrived(1, j, part)

    def weigh_chunk(j):
        q_stage(j).wait()
        q_swap(j, 1 - core).wait_recv()
        arrived_rest(j, 0)

        weigh(j)

    def blend_chunk(j):
        arrived_rest(j, 1)
        blend(j, 1 - core)
        out_remote(j, core).start()
        blend(j, core)
        out_local(j).start()

    def weigh(j):
        for unit in range(2 * GROUP):
            block, h = unit // GROUP, unit % GROUP
            base = 2 * block
            score = sbuf.at[unit % 2]
            q = qbuf[block, j, :, h * HEAD_DIM:(h + 1) * HEAD_DIM]
            upper = (
                lax.broadcasted_iota(jnp.int32, (tok, tok), 1) > lax.broadcasted_iota(jnp.int32, (tok, tok), 0)
            )
            for i in (4, 0, 1, 2, 3):
                s = lax.dot_general(
                    q, kv[base + i, j, 0], (((1,), (1,)), ((), ())), preferred_element_type=jnp.float32
                )
                if i == 4:
                    last = s
                    continue
                s = jnp.where(4 * row + side + base + i >= 4, s, jnp.float32(-1e30))
                if i == 0:
                    s = jnp.where(upper, s, last)
                score[:, i * tok:(i + 1) * tok] = s
            for r in range(0, tok, TILE):
                part = score[r:r + TILE, :]
                top = jnp.max(part, axis=1, keepdims=True)
                expo = jnp.exp2((part - top) * jnp.float32(SCALE_LOG2E))
                weight = expo * (1.0 / jnp.sum(expo, axis=1, keepdims=True))
                rows_here = slice(h * tok + r, h * tok + r + TILE)
                first = weight[:, :tok]
                ahead = (
                    lax.broadcasted_iota(jnp.int32, (TILE, tok), 1)
                    > lax.broadcasted_iota(jnp.int32, (TILE, tok), 0) + r
                )
                wbuf[block, 0, rows_here, :] = jnp.where(ahead, first, 0.0).astype(wbuf.dtype)
                wbuf[block, 4, rows_here, :] = jnp.where(ahead, 0.0, first).astype(wbuf.dtype)
                for i in range(1, 4):
                    wbuf[block, i, rows_here, :] = weight[:, i * tok:(i + 1) * tok].astype(wbuf.dtype)

    def blend(j, block):
        base = 2 * block
        out = None
        for i in range(5):
            term = jnp.dot(wbuf[block, i], kv[base + i, j, 1], preferred_element_type=jnp.float32)
            out = term if out is None else out + term
        out = out.astype(obuf.dtype)
        for h in range(GROUP):
            obuf[block, j, :, h * HEAD_DIM:(h + 1) * HEAD_DIM] = out[h * tok:(h + 1) * tok]

    def out_local(j):
        return pltpu.make_async_copy(
            obuf.at[core, j], o_ref.at[:, cols(core * HALF_KV + j, GROUP * HEAD_DIM)], osem.at[j]
        )

    def out_remote(j, half):
        return pltpu.make_async_remote_copy(
            src_ref=obuf.at[1 - core, j], dst_ref=o_ref.at[:, cols(half * HALF_KV + j, GROUP * HEAD_DIM)],
            send_sem=osend.at[j], recv_sem=orecv.at[j], device_id=partner, device_id_type=MESH,
        )

    for j in range(HALF_KV):
        for part in (0, 1):
            stage(j, part, core).start()
            stage(j, part, 1 - core).start()
        q_stage(j).start()

    barrier = pltpu.get_barrier_semaphore()
    for device in (partner, side_same, side_cross):
        pl.semaphore_signal(barrier, inc=1, device_id=device, device_id_type=MESH)

    @pl.when(has_next)
    def _():
        for device in (next_same, next_cross):
            pl.semaphore_signal(barrier, inc=1, device_id=device, device_id_type=MESH)

    @pl.when(has_prev)
    def _():
        for device in (prev_same, prev_cross):
            pl.semaphore_signal(barrier, inc=1, device_id=device, device_id_type=MESH)

    @pl.when(jnp.logical_not(has_prev))
    def _():
        kv[0:3] = jnp.zeros((3,) + kv.shape[1:], kv.dtype)

        @pl.when(side == 0)
        def _():
            kv[3] = jnp.zeros(kv.shape[1:], kv.dtype)

    pl.semaphore_wait(barrier, 3 + jnp.where(has_next, 2, 0) + jnp.where(has_prev, 2, 0))

    for j, part in ((0, 0), (0, 1), (1, 0)):
        staged(j, part)
        direct_next(j, part, launch)
        direct_side(j, part, launch)
        if part == 0:
            q_swap(j, core).start()
    for j, part in ((1, 1), (2, 0), (2, 1), (3, 0), (3, 1)):
        staged(j, part)
        if part == 0:
            q_swap(j, core).start()

    @pl.when(side == 1)
    def _():
        direct_side(1, 1, launch)
        direct_side(2, 0, launch)

    def step(j, carry):
        @pl.when(j < HALF_KV)
        def _():
            exchange(j, 0)

        @pl.when(j > 0)
        def _():
            weigh_chunk(j - 1)

        @pl.when(j < HALF_KV)
        def _():
            exchange(j, 1)

        @pl.when(j > 0)
        def _():
            blend_chunk(j - 1)

        return carry

    lax.fori_loop(0, HALF_KV + 1, step, 0)

    def finish(j, carry):
        q_swap(j, core).wait_send()
        for part in (0, 1):
            forwards(j, part, lambda copy, slot: None if copy is None else copy.wait_send())
        out_local(j).wait()
        out_remote(j, core).wait_send()
        out_remote(j, 1 - core).wait_recv()
        return carry

    lax.fori_loop(0, HALF_KV, finish, 0)


def fused_body(rows, queries, keys, values):
    tok = queries.shape[0]
    kind = queries.dtype
    wide = GROUP * HEAD_DIM
    dma = pltpu.SemaphoreType.DMA
    return pl.pallas_call(
        functools.partial(fused_kernel, rows),
        out_shape=jax.ShapeDtypeStruct(queries.shape, kind),
        in_specs=[pl.BlockSpec(memory_space=pl.ANY)] * 3,
        out_specs=pl.BlockSpec(memory_space=pl.ANY),
        scratch_shapes=[
            pltpu.VMEM((SLOTS, HALF_KV, 2, tok, HEAD_DIM), kind),
            pltpu.VMEM((HALF_KV, 2, tok, HEAD_DIM), kind),
            pltpu.VMEM((2, HALF_KV, tok, wide), kind),
            pltpu.VMEM((2, tok, WINDOW), jnp.float32),
            pltpu.VMEM((2, 5, GROUP * tok, tok), kind),
            pltpu.VMEM((2, HALF_KV, tok, wide), kind),
            dma((HALF_KV, 4)),
            dma((HALF_KV,)),
            dma((HALF_KV,)),
            dma((HALF_KV,)),
            dma((8, HALF_KV, 2)),
            dma((SLOTS, HALF_KV, 2)),
            dma((HALF_KV,)),
            dma((HALF_KV,)),
            dma((HALF_KV,)),
        ],
        compiler_params=pltpu.CompilerParams(
            collective_id=0, has_side_effects=True, vmem_limit_bytes=58 * 1024 * 1024
        ),
        cost_estimate=pl.CostEstimate(
            flops=4 * tok * HEADS * HEAD_DIM * (WINDOW + tok), bytes_accessed=6 * tok * HEADS * HEAD_DIM,
            transcendentals=tok * HEADS * WINDOW,
        ),
        name="window_attention",
    )(queries, keys, values)


def from_behind(x, axis, by):
    peers = lax.axis_size(axis)
    pairs = [(i, i + by) for i in range(peers) if 0 <= i + by < peers]
    return lax.ppermute(x, axis, pairs)


def attend_block(query_rows, key_win, value_win, block_index):
    tok_rows = query_rows.shape[0]
    span_rows = key_win.shape[0]
    row_ids = jnp.arange(tok_rows, dtype=jnp.int32)[:, None]
    col_ids = jnp.arange(span_rows, dtype=jnp.int32)[None, :]
    position = block_index * tok_rows - WINDOW + col_ids
    allowed = (col_ids > row_ids) & (col_ids <= row_ids + WINDOW) & (position >= 0)

    def head_group(head_index):
        query_part = lax.dynamic_slice_in_dim(query_rows, head_index * GROUP * HEAD_DIM, GROUP * HEAD_DIM, 1)
        query_part = query_part.reshape(tok_rows, GROUP, HEAD_DIM)
        key_part = lax.dynamic_slice_in_dim(key_win, head_index * HEAD_DIM, HEAD_DIM, 1)
        value_part = lax.dynamic_slice_in_dim(value_win, head_index * HEAD_DIM, HEAD_DIM, 1)
        score = jnp.einsum(
            "thd,kd->htk", query_part, key_part, preferred_element_type=jnp.float32
        ) * HEAD_DIM ** (-0.5)
        score = jnp.where(allowed[None], score, jnp.float32(-1e30))
        largest = jnp.max(score, axis=2, keepdims=True)
        expo = jnp.where(allowed[None], jnp.exp(score - largest), jnp.float32(0.0))
        total = jnp.sum(expo, axis=2, keepdims=True)
        weight = (expo / total).astype(jnp.bfloat16)
        output = jnp.einsum("htk,kd->thd", weight, value_part, preferred_element_type=jnp.float32)
        return output.astype(jnp.bfloat16).reshape(tok_rows, GROUP * HEAD_DIM)

    parts = lax.map(head_group, jnp.arange(KV_HEADS, dtype=jnp.int32))
    return jnp.transpose(parts, (1, 0, 2)).reshape(tok_rows, HEADS * HEAD_DIM)


def plain_body(queries, keys, values):
    back_blocks = WINDOW // queries.shape[0]
    block_index = lax.axis_index(("blk", "grp"))
    pieces_k = []
    pieces_v = []
    for offset in range(back_blocks, 0, -1):
        moved_k, moved_v = from_behind((keys, values), ("blk", "grp"), offset)
        pieces_k.append(moved_k)
        pieces_v.append(moved_v)
    key_win = jnp.concatenate(pieces_k + [keys], axis=0)
    value_win = jnp.concatenate(pieces_v + [values], axis=0)
    return attend_block(queries, key_win, value_win, block_index)


def solution(mesh):
    blks, grps = mesh.shape["blk"], mesh.shape["grp"]
    placed = P(("blk", "grp"), None)

    def body(queries, keys, values):
        if grps == 2 and blks % 2 == 0 and 4 * queries.shape[0] == WINDOW:
            return fused_body(blks // 2, queries, keys, values)
        return plain_body(queries, keys, values)

    return jax.shard_map(
        body, mesh=mesh, in_specs=(placed, placed, placed), out_specs=placed, check_vma=False
    )
```

```python
import functools

import jax
import jax.numpy as jnp
from jax import lax
from jax.experimental import pallas as pl
from jax.experimental.pallas import tpu as pltpu
from jax.sharding import PartitionSpec as P

HEADS = 16
KV_HEADS = 8
HEAD_DIM = 128
WINDOW = 1024
GROUP = HEADS // KV_HEADS
HALF_KV = KV_HEADS // 2
SLOTS = 7
TILE = 16
TURNS = 2 * HALF_KV
DEPTH = 3
SCALE_LOG2E = HEAD_DIM ** -0.5 * 1.4426950408889634
MESH = pl.DeviceIdType.MESH


def fused_kernel(
    rows, q_ref, k_ref, v_ref, o_ref, kv, other, qbuf, sbuf, wbuf, obuf,
    stage_sem, qstage_sem, qsend, qrecv, send, recv, osem, osend, orecv,
):
    blk = lax.axis_index("blk")
    side = lax.axis_index("grp")
    row = blk // 2
    core = blk % 2
    tok = q_ref.shape[0]
    has_prev = row > 0
    has_next = row < rows - 1
    own_slot = 4 + 2 * core

    partner = (2 * row + 1 - core, side)
    next_same = (2 * row + 2 + core, side)
    next_cross = (2 * row + 3 - core, side)
    side_same = (2 * row + core, 1 - side)
    side_cross = (2 * row + 1 - core, 1 - side)
    prev_same = (2 * row - 2 + core, side)
    prev_cross = (2 * row - 1 - core, side)

    def cols(index, width):
        return pl.ds(pl.multiple_of(index * width, width), width)

    def stage(j, part, half):
        source = (k_ref, v_ref)[part].at[:, cols(half * HALF_KV + j, HEAD_DIM)]
        if half is core:
            return pltpu.make_async_copy(source, kv.at[own_slot, j, part], stage_sem.at[j, 2 + part])
        return pltpu.make_async_copy(source, other.at[j, part], stage_sem.at[j, part])

    def q_stage(j):
        mine = cols(core * HALF_KV + j, GROUP * HEAD_DIM)
        return pltpu.make_async_copy(q_ref.at[:, mine], qbuf.at[core, j], qstage_sem.at[j])

    def q_swap(j, block):
        rest = cols((1 - core) * HALF_KV + j, GROUP * HEAD_DIM)
        return pltpu.make_async_remote_copy(
            src_ref=q_ref.at[:, rest], dst_ref=qbuf.at[block, j],
            send_sem=qsend.at[j], recv_sem=qrecv.at[j], device_id=partner, device_id_type=MESH,
        )

    def remote(src, dst, kind, arrival, j, part, device):
        return pltpu.make_async_remote_copy(
            src_ref=src, dst_ref=dst, send_sem=send.at[kind, j, part], recv_sem=recv.at[arrival, j, part],
            device_id=device, device_id_type=MESH,
        )

    def piece(slot, j, part):
        return kv.at[slot, j, part]

    def to_partner(j, part):
        return remote(other.at[j, part], piece(own_slot, j, part), 0, own_slot, j, part, partner)

    def to_next(j, part):
        slot = 2 * core
        return [
            remote(piece(own_slot, j, part), piece(slot, j, part), 1, slot, j, part, next_same),
            remote(other.at[j, part], piece(slot, j, part), 2, slot, j, part, next_cross),
        ]

    def to_side(j, part):
        slot = jnp.where(side == 0, 3 + 2 * core, 5)
        return [
            remote(piece(own_slot, j, part), piece(slot, j, part), 3, slot, j, part, side_same),
            remote(other.at[j, part], piece(slot, j, part), 4, slot, j, part, side_cross),
        ]

    sends_side = jnp.logical_or(side == 0, core == 0)

    def pass_side(j, part, slot, to_slot, kind):
        return remote(piece(slot, j, part), piece(to_slot, j, part), kind, to_slot, j, part, side_same)

    def pass_next(j):
        return remote(piece(5, j, 1), piece(1, j, 1), 6, 1, j, 1, next_same)

    def arrived(slot, j, part):
        remote(piece(slot, j, part), piece(slot, j, part), 0, slot, j, part, partner).wait_recv()

    def direct_side(j, part, act):
        @pl.when(sends_side)
        def _():
            for copy in to_side(j, part):
                act(copy)

    def direct_next(j, part, act):
        act(to_partner(j, part))

        @pl.when(has_next)
        def _():
            for copy in to_next(j, part):
                act(copy)

    def forwards(j, part, act):
        @pl.when(jnp.logical_and(has_prev, jnp.logical_and(side == 1, part == 0)))
        def _():
            act(pass_side(j, part, 0, 1, 7), 0)

        @pl.when(jnp.logical_and(has_prev, side == 1))
        def _():
            act(pass_side(j, part, 2, 3, 5), 2)

        @pl.when(jnp.logical_and(has_prev, jnp.logical_and(side == 0, part == 0)))
        def _():
            act(pass_side(j, part, 2, 1, 5), 2)

        @pl.when(jnp.logical_and(has_next, part == 1))
        def _():
            act(pass_next(j), 5)

    def await_kept(j, part):
        @pl.when(jnp.logical_and(has_prev, jnp.logical_or(side == 0, part == 1)))
        def _():
            arrived(0, j, part)

        @pl.when(jnp.logical_and(has_prev, jnp.logical_and(side == 0, part == 1)))
        def _():
            arrived(2, j, part)

        @pl.when(jnp.logical_not(jnp.logical_and(has_next, part == 1)))
        def _():
            arrived(5, j, part)

    def launch(copy):
        copy.start()

    def sent(copy):
        copy.wait_send()

    def staged(j, part):
        stage(j, part, core).wait()
        stage(j, part, 1 - core).wait()

    def turn(t):
        first, last, odd = t == 0, t == TURNS - 1, t % 2 == 1
        part = jnp.where(first, 0, jnp.where(last, 1, 1 - t % 2))
        return jnp.where(first, 0, jnp.where(last, HALF_KV - 1, jnp.where(odd, (t + 1) // 2, t // 2 - 1))), part

    def start_next(t):
        j, part = turn(t)
        direct_next(j, part, launch)

        @pl.when(side == 0)
        def _():
            direct_side(j, part, launch)

    def exchange(t):
        j, part = turn(t)

        def hand_on(copy, slot):
            arrived(slot, j, part)
            copy.start()

        forwards(j, part, hand_on)
        await_kept(j, part)

        @pl.when(t < TURNS - DEPTH)
        def _():
            direct_next(j, part, sent)

            @pl.when(side == 0)
            def _():
                direct_side(j, part, sent)

            start_next(t + DEPTH)

    def arrived_rest(j, part):
        arrived(6 - 2 * core, j, part)

        @pl.when(jnp.logical_or(side == 1, has_prev))
        def _():
            arrived(3, j, part)

        @pl.when(has_prev)
        def _():
            arrived(1, j, part)

    def weigh_chunk(j):
        q_stage(j).wait()
        q_swap(j, 1 - core).wait_recv()
        arrived_rest(j, 0)

        weigh(j)

    def blend_chunk(j):
        arrived_rest(j, 1)
        blend(j, 1 - core)
        out_remote(j, core).start()
        blend(j, core)
        out_local(j).start()

    def weigh(j):
        weights = wbuf.at[j % 2]
        for unit in range(2 * GROUP):
            block, h = unit // GROUP, unit % GROUP
            base = 2 * block
            score = sbuf.at[unit % 2]
            q = qbuf[block, j, :, h * HEAD_DIM:(h + 1) * HEAD_DIM]
            upper = (
                lax.broadcasted_iota(jnp.int32, (tok, tok), 1) > lax.broadcasted_iota(jnp.int32, (tok, tok), 0)
            )
            for i in (4, 0, 1, 2, 3):
                s = lax.dot_general(
                    q, kv[base + i, j, 0], (((1,), (1,)), ((), ())), preferred_element_type=jnp.float32
                )
                if i == 4:
                    last = s
                    continue
                s = jnp.where(4 * row + side + base + i >= 4, s, jnp.float32(-1e30))
                if i == 0:
                    s = jnp.where(upper, s, last)
                score[:, i * tok:(i + 1) * tok] = s
            for r in range(0, tok, TILE):
                part = score[r:r + TILE, :]
                top = jnp.max(part, axis=1, keepdims=True)
                expo = jnp.exp2((part - top) * jnp.float32(SCALE_LOG2E))
                weight = expo * (1.0 / jnp.sum(expo, axis=1, keepdims=True))
                rows_here = slice(h * tok + r, h * tok + r + TILE)
                first = weight[:, :tok]
                ahead = (
                    lax.broadcasted_iota(jnp.int32, (TILE, tok), 1)
                    > lax.broadcasted_iota(jnp.int32, (TILE, tok), 0) + r
                )
                weights[block, 0, rows_here, :] = jnp.where(ahead, first, 0.0).astype(wbuf.dtype)
                weights[block, 4, rows_here, :] = jnp.where(ahead, 0.0, first).astype(wbuf.dtype)
                for i in range(1, 4):
                    weights[block, i, rows_here, :] = weight[:, i * tok:(i + 1) * tok].astype(wbuf.dtype)

    def blend(j, block):
        base = 2 * block
        out = None
        for i in range(5):
            term = jnp.dot(wbuf[j % 2, block, i], kv[base + i, j, 1], preferred_element_type=jnp.float32)
            out = term if out is None else out + term
        out = out.astype(obuf.dtype)
        for h in range(GROUP):
            obuf[block, j, :, h * HEAD_DIM:(h + 1) * HEAD_DIM] = out[h * tok:(h + 1) * tok]

    def out_local(j):
        return pltpu.make_async_copy(
            obuf.at[core, j], o_ref.at[:, cols(core * HALF_KV + j, GROUP * HEAD_DIM)], osem.at[j]
        )

    def out_remote(j, half):
        return pltpu.make_async_remote_copy(
            src_ref=obuf.at[1 - core, j], dst_ref=o_ref.at[:, cols(half * HALF_KV + j, GROUP * HEAD_DIM)],
            send_sem=osend.at[j], recv_sem=orecv.at[j], device_id=partner, device_id_type=MESH,
        )

    for j in range(HALF_KV):
        for part in (0, 1):
            stage(j, part, core).start()
            stage(j, part, 1 - core).start()
        q_stage(j).start()

    barrier = pltpu.get_barrier_semaphore()
    for device in (partner, side_same, side_cross):
        pl.semaphore_signal(barrier, inc=1, device_id=device, device_id_type=MESH)

    @pl.when(has_next)
    def _():
        for device in (next_same, next_cross):
            pl.semaphore_signal(barrier, inc=1, device_id=device, device_id_type=MESH)

    @pl.when(has_prev)
    def _():
        for device in (prev_same, prev_cross):
            pl.semaphore_signal(barrier, inc=1, device_id=device, device_id_type=MESH)

    @pl.when(jnp.logical_not(has_prev))
    def _():
        kv[0:3] = jnp.zeros((3,) + kv.shape[1:], kv.dtype)

        @pl.when(side == 0)
        def _():
            kv[3] = jnp.zeros(kv.shape[1:], kv.dtype)

    pl.semaphore_wait(barrier, 3 + jnp.where(has_next, 2, 0) + jnp.where(has_prev, 2, 0))

    for t, (j, part) in enumerate(((0, 0), (1, 0), (0, 1), (2, 0), (1, 1), (3, 0), (2, 1), (3, 1))):
        staged(j, part)
        if t < DEPTH:
            direct_next(j, part, launch)
            direct_side(j, part, launch)
        else:
            @pl.when(side == 1)
            def _():
                direct_side(j, part, launch)

        if part == 0:
            q_swap(j, core).start()

    def step(t, carry):
        @pl.when(t < TURNS)
        def _():
            exchange(t)

        @pl.when(jnp.logical_or(t == 4, t >= 6))
        def _():
            blend_chunk(jnp.where(t == 4, 0, t - 5))

        @pl.when(jnp.logical_or(t == 2, jnp.logical_and(t >= 4, t <= 6)))
        def _():
            weigh_chunk(jnp.where(t == 2, 0, t - 3))

        return carry

    lax.fori_loop(0, TURNS + 1, step, 0)

    def finish_direct(t, carry):
        j, part = turn(t)
        forwards(j, part, lambda copy, slot: copy.wait_send())

        @pl.when(t >= TURNS - DEPTH)
        def _():
            direct_next(j, part, sent)

        @pl.when(jnp.logical_or(side == 1, t >= TURNS - DEPTH))
        def _():
            direct_side(j, part, sent)

        return carry

    lax.fori_loop(0, TURNS, finish_direct, 0)

    def finish(j, carry):
        q_swap(j, core).wait_send()
        out_local(j).wait()
        out_remote(j, core).wait_send()
        out_remote(j, 1 - core).wait_recv()
        return carry

    lax.fori_loop(0, HALF_KV, finish, 0)


def fused_body(rows, queries, keys, values):
    tok = queries.shape[0]
    kind = queries.dtype
    wide = GROUP * HEAD_DIM
    dma = pltpu.SemaphoreType.DMA
    return pl.pallas_call(
        functools.partial(fused_kernel, rows),
        out_shape=jax.ShapeDtypeStruct(queries.shape, kind),
        in_specs=[pl.BlockSpec(memory_space=pl.ANY)] * 3,
        out_specs=pl.BlockSpec(memory_space=pl.ANY),
        scratch_shapes=[
            pltpu.VMEM((SLOTS, HALF_KV, 2, tok, HEAD_DIM), kind),
            pltpu.VMEM((HALF_KV, 2, tok, HEAD_DIM), kind),
            pltpu.VMEM((2, HALF_KV, tok, wide), kind),
            pltpu.VMEM((2, tok, WINDOW), jnp.float32),
            pltpu.VMEM((2, 2, 5, GROUP * tok, tok), kind),
            pltpu.VMEM((2, HALF_KV, tok, wide), kind),
            dma((HALF_KV, 4)),
            dma((HALF_KV,)),
            dma((HALF_KV,)),
            dma((HALF_KV,)),
            dma((8, HALF_KV, 2)),
            dma((SLOTS, HALF_KV, 2)),
            dma((HALF_KV,)),
            dma((HALF_KV,)),
            dma((HALF_KV,)),
        ],
        compiler_params=pltpu.CompilerParams(
            collective_id=0, has_side_effects=True, vmem_limit_bytes=58 * 1024 * 1024
        ),
        cost_estimate=pl.CostEstimate(
            flops=4 * tok * HEADS * HEAD_DIM * (WINDOW + tok), bytes_accessed=6 * tok * HEADS * HEAD_DIM,
            transcendentals=tok * HEADS * WINDOW,
        ),
        name="window_attention",
    )(queries, keys, values)


def from_behind(x, axis, by):
    peers = lax.axis_size(axis)
    pairs = [(i, i + by) for i in range(peers) if 0 <= i + by < peers]
    return lax.ppermute(x, axis, pairs)


def attend_block(query_rows, key_win, value_win, block_index):
    tok_rows = query_rows.shape[0]
    span_rows = key_win.shape[0]
    row_ids = jnp.arange(tok_rows, dtype=jnp.int32)[:, None]
    col_ids = jnp.arange(span_rows, dtype=jnp.int32)[None, :]
    position = block_index * tok_rows - WINDOW + col_ids
    allowed = (col_ids > row_ids) & (col_ids <= row_ids + WINDOW) & (position >= 0)

    def head_group(head_index):
        query_part = lax.dynamic_slice_in_dim(query_rows, head_index * GROUP * HEAD_DIM, GROUP * HEAD_DIM, 1)
        query_part = query_part.reshape(tok_rows, GROUP, HEAD_DIM)
        key_part = lax.dynamic_slice_in_dim(key_win, head_index * HEAD_DIM, HEAD_DIM, 1)
        value_part = lax.dynamic_slice_in_dim(value_win, head_index * HEAD_DIM, HEAD_DIM, 1)
        score = jnp.einsum(
            "thd,kd->htk", query_part, key_part, preferred_element_type=jnp.float32
        ) * HEAD_DIM ** (-0.5)
        score = jnp.where(allowed[None], score, jnp.float32(-1e30))
        largest = jnp.max(score, axis=2, keepdims=True)
        expo = jnp.where(allowed[None], jnp.exp(score - largest), jnp.float32(0.0))
        total = jnp.sum(expo, axis=2, keepdims=True)
        weight = (expo / total).astype(jnp.bfloat16)
        output = jnp.einsum("htk,kd->thd", weight, value_part, preferred_element_type=jnp.float32)
        return output.astype(jnp.bfloat16).reshape(tok_rows, GROUP * HEAD_DIM)

    parts = lax.map(head_group, jnp.arange(KV_HEADS, dtype=jnp.int32))
    return jnp.transpose(parts, (1, 0, 2)).reshape(tok_rows, HEADS * HEAD_DIM)


def plain_body(queries, keys, values):
    back_blocks = WINDOW // queries.shape[0]
    block_index = lax.axis_index(("blk", "grp"))
    pieces_k = []
    pieces_v = []
    for offset in range(back_blocks, 0, -1):
        moved_k, moved_v = from_behind((keys, values), ("blk", "grp"), offset)
        pieces_k.append(moved_k)
        pieces_v.append(moved_v)
    key_win = jnp.concatenate(pieces_k + [keys], axis=0)
    value_win = jnp.concatenate(pieces_v + [values], axis=0)
    return attend_block(queries, key_win, value_win, block_index)


def solution(mesh):
    blks, grps = mesh.shape["blk"], mesh.shape["grp"]
    placed = P(("blk", "grp"), None)

    def body(queries, keys, values):
        if grps == 2 and blks % 2 == 0 and 4 * queries.shape[0] == WINDOW:
            return fused_body(blks // 2, queries, keys, values)
        return plain_body(queries, keys, values)

    return jax.shard_map(
        body, mesh=mesh, in_specs=(placed, placed, placed), out_specs=placed, check_vma=False
    )
```

```python
import functools

import jax
import jax.numpy as jnp
from jax import lax
from jax.experimental import pallas as pl
from jax.experimental.pallas import tpu as pltpu
from jax.sharding import PartitionSpec as P

HEADS = 16
KV_HEADS = 8
HEAD_DIM = 128
WINDOW = 1024
GROUP = HEADS // KV_HEADS
HALF_KV = KV_HEADS // 2
SLOTS = 7
TILE = 16
TURNS = 2 * HALF_KV
DEPTH = 3
SCALE_LOG2E = HEAD_DIM ** -0.5 * 1.4426950408889634
MESH = pl.DeviceIdType.MESH


def fused_kernel(
    rows, q_ref, k_ref, v_ref, o_ref, kv, other, qbuf, sbuf, wbuf, obuf,
    stage_sem, qstage_sem, qsend, qrecv, send, recv, osem, osend, orecv,
):
    blk = lax.axis_index("blk")
    side = lax.axis_index("grp")
    row = blk // 2
    core = blk % 2
    tok = q_ref.shape[0]
    has_prev = row > 0
    has_next = row < rows - 1
    own_slot = 4 + 2 * core

    partner = (2 * row + 1 - core, side)
    next_same = (2 * row + 2 + core, side)
    next_cross = (2 * row + 3 - core, side)
    side_same = (2 * row + core, 1 - side)
    side_cross = (2 * row + 1 - core, 1 - side)
    prev_same = (2 * row - 2 + core, side)
    prev_cross = (2 * row - 1 - core, side)

    def cols(index, width):
        return pl.ds(pl.multiple_of(index * width, width), width)

    def stage(j, part, half):
        source = (k_ref, v_ref)[part].at[:, cols(half * HALF_KV + j, HEAD_DIM)]
        if half is core:
            return pltpu.make_async_copy(source, kv.at[own_slot, j, part], stage_sem.at[j, 2 + part])
        return pltpu.make_async_copy(source, other.at[j, part], stage_sem.at[j, part])

    def q_stage(j):
        mine = cols(core * HALF_KV + j, GROUP * HEAD_DIM)
        return pltpu.make_async_copy(q_ref.at[:, mine], qbuf.at[core, j], qstage_sem.at[j])

    def q_swap(j, block):
        rest = cols((1 - core) * HALF_KV + j, GROUP * HEAD_DIM)
        return pltpu.make_async_remote_copy(
            src_ref=q_ref.at[:, rest], dst_ref=qbuf.at[block, j],
            send_sem=qsend.at[j], recv_sem=qrecv.at[j], device_id=partner, device_id_type=MESH,
        )

    def remote(src, dst, kind, arrival, j, part, device):
        return pltpu.make_async_remote_copy(
            src_ref=src, dst_ref=dst, send_sem=send.at[kind, j, part], recv_sem=recv.at[arrival, j, part],
            device_id=device, device_id_type=MESH,
        )

    def piece(slot, j, part):
        return kv.at[slot, j, part]

    def to_partner(j, part):
        return remote(other.at[j, part], piece(own_slot, j, part), 0, own_slot, j, part, partner)

    def to_next(j, part):
        slot = 2 * core
        return [
            remote(piece(own_slot, j, part), piece(slot, j, part), 1, slot, j, part, next_same),
            remote(other.at[j, part], piece(slot, j, part), 2, slot, j, part, next_cross),
        ]

    def to_side(j, part):
        slot = jnp.where(side == 0, 3 + 2 * core, 5)
        return [
            remote(piece(own_slot, j, part), piece(slot, j, part), 3, slot, j, part, side_same),
            remote(other.at[j, part], piece(slot, j, part), 4, slot, j, part, side_cross),
        ]

    sends_side = jnp.logical_or(side == 0, core == 0)

    def pass_side(j, part, slot, to_slot, kind):
        return remote(piece(slot, j, part), piece(to_slot, j, part), kind, to_slot, j, part, side_same)

    def pass_next(j):
        return remote(piece(5, j, 1), piece(1, j, 1), 6, 1, j, 1, next_same)

    def arrived(slot, j, part):
        remote(piece(slot, j, part), piece(slot, j, part), 0, slot, j, part, partner).wait_recv()

    def direct_side(j, part, act):
        @pl.when(sends_side)
        def _():
            for copy in to_side(j, part):
                act(copy)

    def direct_next(j, part, act):
        act(to_partner(j, part))

        @pl.when(has_next)
        def _():
            for copy in to_next(j, part):
                act(copy)

    def forwards(j, part, act):
        @pl.when(jnp.logical_and(has_prev, jnp.logical_and(side == 1, part == 0)))
        def _():
            act(pass_side(j, part, 0, 1, 7), 0)

        @pl.when(jnp.logical_and(has_prev, side == 1))
        def _():
            act(pass_side(j, part, 2, 3, 5), 2)

        @pl.when(jnp.logical_and(has_prev, jnp.logical_and(side == 0, part == 0)))
        def _():
            act(pass_side(j, part, 2, 1, 5), 2)

        @pl.when(jnp.logical_and(has_next, part == 1))
        def _():
            act(pass_next(j), 5)

    def await_kept(j, part):
        @pl.when(jnp.logical_and(has_prev, jnp.logical_or(side == 0, part == 1)))
        def _():
            arrived(0, j, part)

        @pl.when(jnp.logical_and(has_prev, jnp.logical_and(side == 0, part == 1)))
        def _():
            arrived(2, j, part)

        @pl.when(jnp.logical_not(jnp.logical_and(has_next, part == 1)))
        def _():
            arrived(5, j, part)

    def launch(copy):
        copy.start()

    def sent(copy):
        copy.wait_send()

    def staged(j, part):
        stage(j, part, core).wait()
        stage(j, part, 1 - core).wait()

    def turn(t):
        first, last, odd = t == 0, t == TURNS - 1, t % 2 == 1
        part = jnp.where(first, 0, jnp.where(last, 1, 1 - t % 2))
        return jnp.where(first, 0, jnp.where(last, HALF_KV - 1, jnp.where(odd, (t + 1) // 2, t // 2 - 1))), part

    def start_next(t):
        j, part = turn(t)
        direct_next(j, part, launch)
        direct_side(j, part, launch)

    def exchange(t):
        j, part = turn(t)

        def hand_on(copy, slot):
            arrived(slot, j, part)
            copy.start()

        forwards(j, part, hand_on)
        await_kept(j, part)

        @pl.when(t < TURNS - DEPTH)
        def _():
            direct_next(j, part, sent)
            direct_side(j, part, sent)
            start_next(t + DEPTH)

    def arrived_rest(j, part):
        arrived(6 - 2 * core, j, part)

        @pl.when(jnp.logical_or(side == 1, has_prev))
        def _():
            arrived(3, j, part)

        @pl.when(has_prev)
        def _():
            arrived(1, j, part)

    def weigh_chunk(j):
        q_stage(j).wait()
        q_swap(j, 1 - core).wait_recv()
        arrived_rest(j, 0)

        weigh(j)

    def blend_chunk(j):
        arrived_rest(j, 1)
        blend(j, 1 - core)
        out_remote(j, core).start()
        blend(j, core)
        out_local(j).start()

    def weigh(j):
        weights = wbuf.at[j % 2]
        for unit in range(2 * GROUP):
            block, h = unit // GROUP, unit % GROUP
            base = 2 * block
            score = sbuf.at[unit % 2]
            q = qbuf[block, j, :, h * HEAD_DIM:(h + 1) * HEAD_DIM]
            upper = (
                lax.broadcasted_iota(jnp.int32, (tok, tok), 1) > lax.broadcasted_iota(jnp.int32, (tok, tok), 0)
            )
            for i in (4, 0, 1, 2, 3):
                s = lax.dot_general(
                    q, kv[base + i, j, 0], (((1,), (1,)), ((), ())), preferred_element_type=jnp.float32
                )
                if i == 4:
                    last = s
                    continue
                s = jnp.where(4 * row + side + base + i >= 4, s, jnp.float32(-1e30))
                if i == 0:
                    s = jnp.where(upper, s, last)
                score[:, i * tok:(i + 1) * tok] = s
            for r in range(0, tok, TILE):
                part = score[r:r + TILE, :]
                top = jnp.max(part, axis=1, keepdims=True)
                expo = jnp.exp2((part - top) * jnp.float32(SCALE_LOG2E))
                weight = expo * (1.0 / jnp.sum(expo, axis=1, keepdims=True))
                rows_here = slice(h * tok + r, h * tok + r + TILE)
                first = weight[:, :tok]
                ahead = (
                    lax.broadcasted_iota(jnp.int32, (TILE, tok), 1)
                    > lax.broadcasted_iota(jnp.int32, (TILE, tok), 0) + r
                )
                weights[block, 0, rows_here, :] = jnp.where(ahead, first, 0.0).astype(wbuf.dtype)
                weights[block, 4, rows_here, :] = jnp.where(ahead, 0.0, first).astype(wbuf.dtype)
                for i in range(1, 4):
                    weights[block, i, rows_here, :] = weight[:, i * tok:(i + 1) * tok].astype(wbuf.dtype)

    def blend(j, block):
        base = 2 * block
        out = None
        for i in range(5):
            term = jnp.dot(wbuf[j % 2, block, i], kv[base + i, j, 1], preferred_element_type=jnp.float32)
            out = term if out is None else out + term
        out = out.astype(obuf.dtype)
        for h in range(GROUP):
            obuf[block, j, :, h * HEAD_DIM:(h + 1) * HEAD_DIM] = out[h * tok:(h + 1) * tok]

    def out_local(j):
        return pltpu.make_async_copy(
            obuf.at[core, j], o_ref.at[:, cols(core * HALF_KV + j, GROUP * HEAD_DIM)], osem.at[j]
        )

    def out_remote(j, half):
        return pltpu.make_async_remote_copy(
            src_ref=obuf.at[1 - core, j], dst_ref=o_ref.at[:, cols(half * HALF_KV + j, GROUP * HEAD_DIM)],
            send_sem=osend.at[j], recv_sem=orecv.at[j], device_id=partner, device_id_type=MESH,
        )

    for j in range(HALF_KV):
        for part in (0, 1):
            stage(j, part, core).start()
            stage(j, part, 1 - core).start()
        q_stage(j).start()

    barrier = pltpu.get_barrier_semaphore()
    for device in (partner, side_same, side_cross):
        pl.semaphore_signal(barrier, inc=1, device_id=device, device_id_type=MESH)

    @pl.when(has_next)
    def _():
        for device in (next_same, next_cross):
            pl.semaphore_signal(barrier, inc=1, device_id=device, device_id_type=MESH)

    @pl.when(has_prev)
    def _():
        for device in (prev_same, prev_cross):
            pl.semaphore_signal(barrier, inc=1, device_id=device, device_id_type=MESH)

    @pl.when(jnp.logical_not(has_prev))
    def _():
        kv[0:3] = jnp.zeros((3,) + kv.shape[1:], kv.dtype)

        @pl.when(side == 0)
        def _():
            kv[3] = jnp.zeros(kv.shape[1:], kv.dtype)

    pl.semaphore_wait(barrier, 3 + jnp.where(has_next, 2, 0) + jnp.where(has_prev, 2, 0))

    for t, (j, part) in enumerate(((0, 0), (1, 0), (0, 1), (2, 0), (1, 1), (3, 0), (2, 1), (3, 1))):
        staged(j, part)
        if t < DEPTH:
            direct_next(j, part, launch)
            direct_side(j, part, launch)
        if part == 0:
            q_swap(j, core).start()

    def step(t, carry):
        @pl.when(t < TURNS)
        def _():
            exchange(t)

        @pl.when(jnp.logical_or(t == 4, t >= 6))
        def _():
            blend_chunk(jnp.where(t == 4, 0, t - 5))

        @pl.when(jnp.logical_or(jnp.logical_or(t == 2, t == 4), jnp.logical_or(t == 5, t == 7)))
        def _():
            weigh_chunk(jnp.where(t == 2, 0, jnp.where(t == 7, 3, t - 3)))

        return carry

    lax.fori_loop(0, TURNS + 1, step, 0)

    def finish_direct(t, carry):
        j, part = turn(t)
        forwards(j, part, lambda copy, slot: copy.wait_send())

        @pl.when(t >= TURNS - DEPTH)
        def _():
            direct_next(j, part, sent)
            direct_side(j, part, sent)

        return carry

    lax.fori_loop(0, TURNS, finish_direct, 0)

    def finish(j, carry):
        q_swap(j, core).wait_send()
        out_local(j).wait()
        out_remote(j, core).wait_send()
        out_remote(j, 1 - core).wait_recv()
        return carry

    lax.fori_loop(0, HALF_KV, finish, 0)


def fused_body(rows, queries, keys, values):
    tok = queries.shape[0]
    kind = queries.dtype
    wide = GROUP * HEAD_DIM
    dma = pltpu.SemaphoreType.DMA
    return pl.pallas_call(
        functools.partial(fused_kernel, rows),
        out_shape=jax.ShapeDtypeStruct(queries.shape, kind),
        in_specs=[pl.BlockSpec(memory_space=pl.ANY)] * 3,
        out_specs=pl.BlockSpec(memory_space=pl.ANY),
        scratch_shapes=[
            pltpu.VMEM((SLOTS, HALF_KV, 2, tok, HEAD_DIM), kind),
            pltpu.VMEM((HALF_KV, 2, tok, HEAD_DIM), kind),
            pltpu.VMEM((2, HALF_KV, tok, wide), kind),
            pltpu.VMEM((2, tok, WINDOW), jnp.float32),
            pltpu.VMEM((2, 2, 5, GROUP * tok, tok), kind),
            pltpu.VMEM((2, HALF_KV, tok, wide), kind),
            dma((HALF_KV, 4)),
            dma((HALF_KV,)),
            dma((HALF_KV,)),
            dma((HALF_KV,)),
            dma((8, HALF_KV, 2)),
            dma((SLOTS, HALF_KV, 2)),
            dma((HALF_KV,)),
            dma((HALF_KV,)),
            dma((HALF_KV,)),
        ],
        compiler_params=pltpu.CompilerParams(
            collective_id=0, has_side_effects=True, vmem_limit_bytes=58 * 1024 * 1024
        ),
        cost_estimate=pl.CostEstimate(
            flops=4 * tok * HEADS * HEAD_DIM * (WINDOW + tok), bytes_accessed=6 * tok * HEADS * HEAD_DIM,
            transcendentals=tok * HEADS * WINDOW,
        ),
        name="window_attention",
    )(queries, keys, values)


def from_behind(x, axis, by):
    peers = lax.axis_size(axis)
    pairs = [(i, i + by) for i in range(peers) if 0 <= i + by < peers]
    return lax.ppermute(x, axis, pairs)


def attend_block(query_rows, key_win, value_win, block_index):
    tok_rows = query_rows.shape[0]
    span_rows = key_win.shape[0]
    row_ids = jnp.arange(tok_rows, dtype=jnp.int32)[:, None]
    col_ids = jnp.arange(span_rows, dtype=jnp.int32)[None, :]
    position = block_index * tok_rows - WINDOW + col_ids
    allowed = (col_ids > row_ids) & (col_ids <= row_ids + WINDOW) & (position >= 0)

    def head_group(head_index):
        query_part = lax.dynamic_slice_in_dim(query_rows, head_index * GROUP * HEAD_DIM, GROUP * HEAD_DIM, 1)
        query_part = query_part.reshape(tok_rows, GROUP, HEAD_DIM)
        key_part = lax.dynamic_slice_in_dim(key_win, head_index * HEAD_DIM, HEAD_DIM, 1)
        value_part = lax.dynamic_slice_in_dim(value_win, head_index * HEAD_DIM, HEAD_DIM, 1)
        score = jnp.einsum(
            "thd,kd->htk", query_part, key_part, preferred_element_type=jnp.float32
        ) * HEAD_DIM ** (-0.5)
        score = jnp.where(allowed[None], score, jnp.float32(-1e30))
        largest = jnp.max(score, axis=2, keepdims=True)
        expo = jnp.where(allowed[None], jnp.exp(score - largest), jnp.float32(0.0))
        total = jnp.sum(expo, axis=2, keepdims=True)
        weight = (expo / total).astype(jnp.bfloat16)
        output = jnp.einsum("htk,kd->thd", weight, value_part, preferred_element_type=jnp.float32)
        return output.astype(jnp.bfloat16).reshape(tok_rows, GROUP * HEAD_DIM)

    parts = lax.map(head_group, jnp.arange(KV_HEADS, dtype=jnp.int32))
    return jnp.transpose(parts, (1, 0, 2)).reshape(tok_rows, HEADS * HEAD_DIM)


def plain_body(queries, keys, values):
    back_blocks = WINDOW // queries.shape[0]
    block_index = lax.axis_index(("blk", "grp"))
    pieces_k = []
    pieces_v = []
    for offset in range(back_blocks, 0, -1):
        moved_k, moved_v = from_behind((keys, values), ("blk", "grp"), offset)
        pieces_k.append(moved_k)
        pieces_v.append(moved_v)
    key_win = jnp.concatenate(pieces_k + [keys], axis=0)
    value_win = jnp.concatenate(pieces_v + [values], axis=0)
    return attend_block(queries, key_win, value_win, block_index)


def solution(mesh):
    blks, grps = mesh.shape["blk"], mesh.shape["grp"]
    placed = P(("blk", "grp"), None)

    def body(queries, keys, values):
        if grps == 2 and blks % 2 == 0 and 4 * queries.shape[0] == WINDOW:
            return fused_body(blks // 2, queries, keys, values)
        return plain_body(queries, keys, values)

    return jax.shard_map(
        body, mesh=mesh, in_specs=(placed, placed, placed), out_specs=placed, check_vma=False
    )
```

```python
import functools

import jax
import jax.numpy as jnp
from jax import lax
from jax.experimental import pallas as pl
from jax.experimental.pallas import tpu as pltpu
from jax.sharding import PartitionSpec as P

HEADS = 16
KV_HEADS = 8
HEAD_DIM = 128
WINDOW = 1024
GROUP = HEADS // KV_HEADS
HALF_KV = KV_HEADS // 2
SLOTS = 7
TILE = 16
TURNS = 2 * HALF_KV
DEPTH = 3
SCALE_LOG2E = HEAD_DIM ** -0.5 * 1.4426950408889634
MESH = pl.DeviceIdType.MESH


def fused_kernel(
    rows, q_ref, k_ref, v_ref, o_ref, kv, other, qbuf, sbuf, wbuf, obuf,
    stage_sem, qstage_sem, qsend, qrecv, send, recv, osem, osend, orecv,
):
    blk = lax.axis_index("blk")
    side = lax.axis_index("grp")
    row = blk // 2
    core = blk % 2
    tok = q_ref.shape[0]
    has_prev = row > 0
    has_next = row < rows - 1
    own_slot = 4 + 2 * core

    partner = (2 * row + 1 - core, side)
    next_same = (2 * row + 2 + core, side)
    next_cross = (2 * row + 3 - core, side)
    side_same = (2 * row + core, 1 - side)
    side_cross = (2 * row + 1 - core, 1 - side)
    prev_same = (2 * row - 2 + core, side)
    prev_cross = (2 * row - 1 - core, side)

    def cols(index, width):
        return pl.ds(pl.multiple_of(index * width, width), width)

    def stage(j, part, half):
        source = (k_ref, v_ref)[part].at[:, cols(half * HALF_KV + j, HEAD_DIM)]
        if half is core:
            return pltpu.make_async_copy(source, kv.at[own_slot, j, part], stage_sem.at[j, 2 + part])
        return pltpu.make_async_copy(source, other.at[j, part], stage_sem.at[j, part])

    def q_stage(j):
        mine = cols(core * HALF_KV + j, GROUP * HEAD_DIM)
        return pltpu.make_async_copy(q_ref.at[:, mine], qbuf.at[core, j], qstage_sem.at[j])

    def q_swap(j, block):
        rest = cols((1 - core) * HALF_KV + j, GROUP * HEAD_DIM)
        return pltpu.make_async_remote_copy(
            src_ref=q_ref.at[:, rest], dst_ref=qbuf.at[block, j],
            send_sem=qsend.at[j], recv_sem=qrecv.at[j], device_id=partner, device_id_type=MESH,
        )

    def remote(src, dst, kind, arrival, j, part, device):
        return pltpu.make_async_remote_copy(
            src_ref=src, dst_ref=dst, send_sem=send.at[kind, j, part], recv_sem=recv.at[arrival, j, part],
            device_id=device, device_id_type=MESH,
        )

    def piece(slot, j, part):
        return kv.at[slot, j, part]

    def to_partner(j, part):
        return remote(other.at[j, part], piece(own_slot, j, part), 0, own_slot, j, part, partner)

    def to_next(j, part):
        slot = 2 * core
        return [
            remote(piece(own_slot, j, part), piece(slot, j, part), 1, slot, j, part, next_same),
            remote(other.at[j, part], piece(slot, j, part), 2, slot, j, part, next_cross),
        ]

    def to_side(j, part):
        slot = jnp.where(side == 0, 3 + 2 * core, 5)
        return [
            remote(piece(own_slot, j, part), piece(slot, j, part), 3, slot, j, part, side_same),
            remote(other.at[j, part], piece(slot, j, part), 4, slot, j, part, side_cross),
        ]

    sends_side = jnp.logical_or(side == 0, core == 0)

    def pass_side(j, part, slot, to_slot, kind):
        return remote(piece(slot, j, part), piece(to_slot, j, part), kind, to_slot, j, part, side_same)

    def pass_next(j):
        return remote(piece(5, j, 1), piece(1, j, 1), 6, 1, j, 1, next_same)

    def arrived(slot, j, part):
        remote(piece(slot, j, part), piece(slot, j, part), 0, slot, j, part, partner).wait_recv()

    def direct_side(j, part, act):
        @pl.when(sends_side)
        def _():
            for copy in to_side(j, part):
                act(copy)

    def direct_next(j, part, act):
        act(to_partner(j, part))

        @pl.when(has_next)
        def _():
            for copy in to_next(j, part):
                act(copy)

    def forwards(j, part, act):
        @pl.when(jnp.logical_and(has_prev, jnp.logical_and(side == 1, part == 0)))
        def _():
            act(pass_side(j, part, 0, 1, 7), 0)

        @pl.when(jnp.logical_and(has_prev, side == 1))
        def _():
            act(pass_side(j, part, 2, 3, 5), 2)

        @pl.when(jnp.logical_and(has_prev, jnp.logical_and(side == 0, part == 0)))
        def _():
            act(pass_side(j, part, 2, 1, 5), 2)

        @pl.when(jnp.logical_and(has_next, part == 1))
        def _():
            act(pass_next(j), 5)

    def await_kept(j, part):
        @pl.when(jnp.logical_and(has_prev, jnp.logical_or(side == 0, part == 1)))
        def _():
            arrived(0, j, part)

        @pl.when(jnp.logical_and(has_prev, jnp.logical_and(side == 0, part == 1)))
        def _():
            arrived(2, j, part)

        @pl.when(jnp.logical_not(jnp.logical_and(has_next, part == 1)))
        def _():
            arrived(5, j, part)

    def launch(copy):
        copy.start()

    def sent(copy):
        copy.wait_send()

    def staged(j, part):
        stage(j, part, core).wait()
        stage(j, part, 1 - core).wait()

    def turn(t):
        first, last, odd = t == 0, t == TURNS - 1, t % 2 == 1
        part = jnp.where(first, 0, jnp.where(last, 1, 1 - t % 2))
        return jnp.where(first, 0, jnp.where(last, HALF_KV - 1, jnp.where(odd, (t + 1) // 2, t // 2 - 1))), part

    def start_next(t):
        j, part = turn(t)
        direct_next(j, part, launch)

        @pl.when(side == 0)
        def _():
            direct_side(j, part, launch)

    def start_side(t):
        j, part = turn(t)

        @pl.when(jnp.logical_and(side == 1, t < TURNS))
        def _():
            direct_side(j, part, launch)

    def exchange(t):
        j, part = turn(t)

        def hand_on(copy, slot):
            arrived(slot, j, part)
            copy.start()

        forwards(j, part, hand_on)
        await_kept(j, part)

        @pl.when(t < TURNS - DEPTH)
        def _():
            @pl.when(t > 0)
            def _():
                direct_next(j, part, sent)
                direct_side(j, part, sent)

            @pl.when(t == 0)
            def _():
                start_next(DEPTH - 1)

            start_next(t + DEPTH)
            start_side(t + DEPTH + 1)

    def arrived_rest(j, part):
        arrived(6 - 2 * core, j, part)

        @pl.when(jnp.logical_or(side == 1, has_prev))
        def _():
            arrived(3, j, part)

        @pl.when(has_prev)
        def _():
            arrived(1, j, part)

    def weigh_chunk(j):
        q_stage(j).wait()
        q_swap(j, 1 - core).wait_recv()
        arrived_rest(j, 0)

        weigh(j)

    def blend_chunk(j):
        arrived_rest(j, 1)
        blend(j, 1 - core)
        out_remote(j, core).start()
        blend(j, core)
        out_local(j).start()

    def weigh(j):
        weights = wbuf.at[j % 2]
        for unit in range(2 * GROUP):
            block, h = unit // GROUP, unit % GROUP
            base = 2 * block
            score = sbuf.at[unit % 2]
            q = qbuf[block, j, :, h * HEAD_DIM:(h + 1) * HEAD_DIM]
            upper = (
                lax.broadcasted_iota(jnp.int32, (tok, tok), 1) > lax.broadcasted_iota(jnp.int32, (tok, tok), 0)
            )
            for i in (4, 0, 1, 2, 3):
                s = lax.dot_general(
                    q, kv[base + i, j, 0], (((1,), (1,)), ((), ())), preferred_element_type=jnp.float32
                )
                if i == 4:
                    last = s
                    continue
                s = jnp.where(4 * row + side + base + i >= 4, s, jnp.float32(-1e30))
                if i == 0:
                    s = jnp.where(upper, s, last)
                score[:, i * tok:(i + 1) * tok] = s
            for r in range(0, tok, TILE):
                part = score[r:r + TILE, :]
                top = jnp.max(part, axis=1, keepdims=True)
                expo = jnp.exp2((part - top) * jnp.float32(SCALE_LOG2E))
                weight = expo * (1.0 / jnp.sum(expo, axis=1, keepdims=True))
                rows_here = slice(h * tok + r, h * tok + r + TILE)
                first = weight[:, :tok]
                ahead = (
                    lax.broadcasted_iota(jnp.int32, (TILE, tok), 1)
                    > lax.broadcasted_iota(jnp.int32, (TILE, tok), 0) + r
                )
                weights[block, 0, rows_here, :] = jnp.where(ahead, first, 0.0).astype(wbuf.dtype)
                weights[block, 4, rows_here, :] = jnp.where(ahead, 0.0, first).astype(wbuf.dtype)
                for i in range(1, 4):
                    weights[block, i, rows_here, :] = weight[:, i * tok:(i + 1) * tok].astype(wbuf.dtype)

    def blend(j, block):
        base = 2 * block
        out = None
        for i in range(5):
            term = jnp.dot(wbuf[j % 2, block, i], kv[base + i, j, 1], preferred_element_type=jnp.float32)
            out = term if out is None else out + term
        out = out.astype(obuf.dtype)
        for h in range(GROUP):
            obuf[block, j, :, h * HEAD_DIM:(h + 1) * HEAD_DIM] = out[h * tok:(h + 1) * tok]

    def out_local(j):
        return pltpu.make_async_copy(
            obuf.at[core, j], o_ref.at[:, cols(core * HALF_KV + j, GROUP * HEAD_DIM)], osem.at[j]
        )

    def out_remote(j, half):
        return pltpu.make_async_remote_copy(
            src_ref=obuf.at[1 - core, j], dst_ref=o_ref.at[:, cols(half * HALF_KV + j, GROUP * HEAD_DIM)],
            send_sem=osend.at[j], recv_sem=orecv.at[j], device_id=partner, device_id_type=MESH,
        )

    for j in range(HALF_KV):
        for part in (0, 1):
            stage(j, part, core).start()
            stage(j, part, 1 - core).start()
        q_stage(j).start()

    barrier = pltpu.get_barrier_semaphore()
    for device in (partner, side_same, side_cross):
        pl.semaphore_signal(barrier, inc=1, device_id=device, device_id_type=MESH)

    @pl.when(has_next)
    def _():
        for device in (next_same, next_cross):
            pl.semaphore_signal(barrier, inc=1, device_id=device, device_id_type=MESH)

    @pl.when(has_prev)
    def _():
        for device in (prev_same, prev_cross):
            pl.semaphore_signal(barrier, inc=1, device_id=device, device_id_type=MESH)

    @pl.when(jnp.logical_not(has_prev))
    def _():
        kv[0:3] = jnp.zeros((3,) + kv.shape[1:], kv.dtype)

        @pl.when(side == 0)
        def _():
            kv[3] = jnp.zeros(kv.shape[1:], kv.dtype)

    pl.semaphore_wait(barrier, 3 + jnp.where(has_next, 2, 0) + jnp.where(has_prev, 2, 0))

    for t, (j, part) in enumerate(((0, 0), (1, 0), (0, 1), (2, 0), (1, 1), (3, 0), (2, 1), (3, 1))):
        staged(j, part)
        if t < DEPTH - 1:
            direct_next(j, part, launch)
            direct_side(j, part, launch)
        elif t < DEPTH + 1:
            start_side(t)

        if part == 0:
            q_swap(j, core).start()

    def step(t, carry):
        @pl.when(t < TURNS)
        def _():
            exchange(t)

        @pl.when(jnp.logical_or(t == 4, t >= 6))
        def _():
            blend_chunk(jnp.where(t == 4, 0, t - 5))

        @pl.when(jnp.logical_or(jnp.logical_or(t == 2, t == 4), jnp.logical_or(t == 5, t == 7)))
        def _():
            weigh_chunk(jnp.where(t == 2, 0, jnp.where(t == 7, 3, t - 3)))

        return carry

    lax.fori_loop(0, TURNS + 1, step, 0)

    def finish_direct(t, carry):
        j, part = turn(t)
        forwards(j, part, lambda copy, slot: copy.wait_send())

        @pl.when(jnp.logical_or(t == 0, t >= TURNS - DEPTH))
        def _():
            direct_next(j, part, sent)
            direct_side(j, part, sent)

        return carry

    lax.fori_loop(0, TURNS, finish_direct, 0)

    def finish(j, carry):
        q_swap(j, core).wait_send()
        out_local(j).wait()
        out_remote(j, core).wait_send()
        out_remote(j, 1 - core).wait_recv()
        return carry

    lax.fori_loop(0, HALF_KV, finish, 0)


def fused_body(rows, queries, keys, values):
    tok = queries.shape[0]
    kind = queries.dtype
    wide = GROUP * HEAD_DIM
    dma = pltpu.SemaphoreType.DMA
    return pl.pallas_call(
        functools.partial(fused_kernel, rows),
        out_shape=jax.ShapeDtypeStruct(queries.shape, kind),
        in_specs=[pl.BlockSpec(memory_space=pl.ANY)] * 3,
        out_specs=pl.BlockSpec(memory_space=pl.ANY),
        scratch_shapes=[
            pltpu.VMEM((SLOTS, HALF_KV, 2, tok, HEAD_DIM), kind),
            pltpu.VMEM((HALF_KV, 2, tok, HEAD_DIM), kind),
            pltpu.VMEM((2, HALF_KV, tok, wide), kind),
            pltpu.VMEM((2, tok, WINDOW), jnp.float32),
            pltpu.VMEM((2, 2, 5, GROUP * tok, tok), kind),
            pltpu.VMEM((2, HALF_KV, tok, wide), kind),
            dma((HALF_KV, 4)),
            dma((HALF_KV,)),
            dma((HALF_KV,)),
            dma((HALF_KV,)),
            dma((8, HALF_KV, 2)),
            dma((SLOTS, HALF_KV, 2)),
            dma((HALF_KV,)),
            dma((HALF_KV,)),
            dma((HALF_KV,)),
        ],
        compiler_params=pltpu.CompilerParams(
            collective_id=0, has_side_effects=True, vmem_limit_bytes=40 * 1024 * 1024
        ),
        cost_estimate=pl.CostEstimate(
            flops=4 * tok * HEADS * HEAD_DIM * (WINDOW + tok), bytes_accessed=6 * tok * HEADS * HEAD_DIM,
            transcendentals=tok * HEADS * WINDOW,
        ),
        name="window_attention",
    )(*(pltpu.with_memory_space_constraint(x, pltpu.HBM) for x in (queries, keys, values)))


def from_behind(x, axis, by):
    peers = lax.axis_size(axis)
    pairs = [(i, i + by) for i in range(peers) if 0 <= i + by < peers]
    return lax.ppermute(x, axis, pairs)


def attend_block(query_rows, key_win, value_win, block_index):
    tok_rows = query_rows.shape[0]
    span_rows = key_win.shape[0]
    row_ids = jnp.arange(tok_rows, dtype=jnp.int32)[:, None]
    col_ids = jnp.arange(span_rows, dtype=jnp.int32)[None, :]
    position = block_index * tok_rows - WINDOW + col_ids
    allowed = (col_ids > row_ids) & (col_ids <= row_ids + WINDOW) & (position >= 0)

    def head_group(head_index):
        query_part = lax.dynamic_slice_in_dim(query_rows, head_index * GROUP * HEAD_DIM, GROUP * HEAD_DIM, 1)
        query_part = query_part.reshape(tok_rows, GROUP, HEAD_DIM)
        key_part = lax.dynamic_slice_in_dim(key_win, head_index * HEAD_DIM, HEAD_DIM, 1)
        value_part = lax.dynamic_slice_in_dim(value_win, head_index * HEAD_DIM, HEAD_DIM, 1)
        score = jnp.einsum(
            "thd,kd->htk", query_part, key_part, preferred_element_type=jnp.float32
        ) * HEAD_DIM ** (-0.5)
        score = jnp.where(allowed[None], score, jnp.float32(-1e30))
        largest = jnp.max(score, axis=2, keepdims=True)
        expo = jnp.where(allowed[None], jnp.exp(score - largest), jnp.float32(0.0))
        total = jnp.sum(expo, axis=2, keepdims=True)
        weight = (expo / total).astype(jnp.bfloat16)
        output = jnp.einsum("htk,kd->thd", weight, value_part, preferred_element_type=jnp.float32)
        return output.astype(jnp.bfloat16).reshape(tok_rows, GROUP * HEAD_DIM)

    parts = lax.map(head_group, jnp.arange(KV_HEADS, dtype=jnp.int32))
    return jnp.transpose(parts, (1, 0, 2)).reshape(tok_rows, HEADS * HEAD_DIM)


def plain_body(queries, keys, values):
    back_blocks = WINDOW // queries.shape[0]
    block_index = lax.axis_index(("blk", "grp"))
    pieces_k = []
    pieces_v = []
    for offset in range(back_blocks, 0, -1):
        moved_k, moved_v = from_behind((keys, values), ("blk", "grp"), offset)
        pieces_k.append(moved_k)
        pieces_v.append(moved_v)
    key_win = jnp.concatenate(pieces_k + [keys], axis=0)
    value_win = jnp.concatenate(pieces_v + [values], axis=0)
    return attend_block(queries, key_win, value_win, block_index)


def solution(mesh):
    blks, grps = mesh.shape["blk"], mesh.shape["grp"]
    placed = P(("blk", "grp"), None)

    def body(queries, keys, values):
        if grps == 2 and blks % 2 == 0 and 4 * queries.shape[0] == WINDOW:
            return fused_body(blks // 2, queries, keys, values)
        return plain_body(queries, keys, values)

    return jax.shard_map(
        body, mesh=mesh, in_specs=(placed, placed, placed), out_specs=placed, check_vma=False
    )
```

```python
import functools

import jax
import jax.numpy as jnp
from jax import lax
from jax.experimental import pallas as pl
from jax.experimental.pallas import tpu as pltpu
from jax.sharding import PartitionSpec as P

HEADS = 16
KV_HEADS = 8
HEAD_DIM = 128
WINDOW = 1024
GROUP = HEADS // KV_HEADS
HALF_KV = KV_HEADS // 2
SLOTS = 7
TILE = 16
SCALE_LOG2E = HEAD_DIM ** -0.5 * 1.4426950408889634
MESH = pl.DeviceIdType.MESH


def fused_kernel(
    rows, q_ref, k_ref, v_ref, o_ref, kv, other, qbuf, sbuf, wbuf, obuf,
    stage_sem, qstage_sem, qsend, qrecv, send, recv, osem, osend, orecv,
):
    blk = lax.axis_index("blk")
    side = lax.axis_index("grp")
    row = blk // 2
    core = blk % 2
    tok = q_ref.shape[0]
    has_prev = row > 0
    has_next = row < rows - 1
    own_slot = 4 + 2 * core

    partner = (2 * row + 1 - core, side)
    next_same = (2 * row + 2 + core, side)
    next_cross = (2 * row + 3 - core, side)
    side_same = (2 * row + core, 1 - side)
    side_cross = (2 * row + 1 - core, 1 - side)
    prev_same = (2 * row - 2 + core, side)
    prev_cross = (2 * row - 1 - core, side)

    def cols(index, width):
        return pl.ds(pl.multiple_of(index * width, width), width)

    def stage(j, part, half):
        source = (k_ref, v_ref)[part].at[:, cols(half * HALF_KV + j, HEAD_DIM)]
        if half is core:
            return pltpu.make_async_copy(source, kv.at[own_slot, j, part], stage_sem.at[j, 2 + part])
        return pltpu.make_async_copy(source, other.at[j, part], stage_sem.at[j, part])

    def q_stage(j):
        mine = cols(core * HALF_KV + j, GROUP * HEAD_DIM)
        return pltpu.make_async_copy(q_ref.at[:, mine], qbuf.at[core, j], qstage_sem.at[j])

    def q_swap(j, block):
        rest = cols((1 - core) * HALF_KV + j, GROUP * HEAD_DIM)
        return pltpu.make_async_remote_copy(
            src_ref=q_ref.at[:, rest], dst_ref=qbuf.at[block, j],
            send_sem=qsend.at[j], recv_sem=qrecv.at[j], device_id=partner, device_id_type=MESH,
        )

    def remote(src, dst, kind, arrival, j, part, device):
        return pltpu.make_async_remote_copy(
            src_ref=src, dst_ref=dst, send_sem=send.at[kind, j, part], recv_sem=recv.at[arrival, j, part],
            device_id=device, device_id_type=MESH,
        )

    def piece(slot, j, part):
        return kv.at[slot, j, part]

    def to_partner(j, part):
        return remote(other.at[j, part], piece(own_slot, j, part), 0, own_slot, j, part, partner)

    def to_next(j, part):
        slot = 2 * core
        return [
            remote(piece(own_slot, j, part), piece(slot, j, part), 1, slot, j, part, next_same),
            remote(other.at[j, part], piece(slot, j, part), 2, slot, j, part, next_cross),
        ]

    def to_side(j, part):
        slot = jnp.where(side == 0, 3 + 2 * core, 5)
        return [
            remote(piece(own_slot, j, part), piece(slot, j, part), 3, slot, j, part, side_same),
            remote(other.at[j, part], piece(slot, j, part), 4, slot, j, part, side_cross),
        ]

    sends_side = jnp.logical_or(side == 0, core == 0)

    def pass_side(j, part, slot, to_slot, kind):
        return remote(piece(slot, j, part), piece(to_slot, j, part), kind, to_slot, j, part, side_same)

    def pass_next(j):
        return remote(piece(5, j, 1), piece(1, j, 1), 6, 1, j, 1, next_same)

    def arrived(slot, j, part):
        remote(piece(slot, j, part), piece(slot, j, part), 0, slot, j, part, partner).wait_recv()

    def direct_side(j, part, act):
        @pl.when(sends_side)
        def _():
            for copy in to_side(j, part):
                act(copy)

    def direct_next(j, part, act):
        act(to_partner(j, part))

        @pl.when(has_next)
        def _():
            for copy in to_next(j, part):
                act(copy)

    def forwards(j, part, act):
        @pl.when(jnp.logical_and(has_prev, side == 1))
        def _():
            act(pass_side(j, part, 2, 3, 5), 2)
            if part == 0:
                act(pass_side(j, part, 0, 1, 7), 0)
            else:
                act(None, 0)

        @pl.when(jnp.logical_and(has_prev, side == 0))
        def _():
            act(pass_side(j, part, 2, 1, 5) if part == 0 else None, 2)
            act(None, 0)

        if part == 0:
            act(None, 5)
        else:
            @pl.when(has_next)
            def _():
                act(pass_next(j), 5)

            @pl.when(jnp.logical_not(has_next))
            def _():
                act(None, 5)

    def launch(copy):
        copy.start()

    def sent(copy):
        copy.wait_send()

    def staged(j, part):
        stage(j, part, core).wait()
        stage(j, part, 1 - core).wait()

    def exchange(j, part):
        def hand_on(copy, slot):
            arrived(slot, j, part)
            if copy is not None:
                copy.start()

        forwards(j, part, hand_on)
        direct_side(j, part, sent)
        direct_next(j, part, sent)

        @pl.when(j < HALF_KV - 1 - part)
        def _():
            direct_next(j + 1 + part, 1 - part, launch)

        @pl.when(jnp.logical_and(side == 0, j < HALF_KV - 1 - part))
        def _():
            direct_side(j + 1 + part, 1 - part, launch)

        @pl.when(jnp.logical_and(side == 1, j < HALF_KV - 2 - part))
        def _():
            direct_side(j + 2 + part, 1 - part, launch)

    def arrived_rest(j, part):
        arrived(6 - 2 * core, j, part)

        @pl.when(jnp.logical_or(side == 1, has_prev))
        def _():
            arrived(3, j, part)

        @pl.when(has_prev)
        def _():
            arrived(1, j, part)

    def weigh_chunk(j):
        q_stage(j).wait()
        q_swap(j, 1 - core).wait_recv()
        arrived_rest(j, 0)

        weigh(j)

    def blend_chunk(j):
        arrived_rest(j, 1)
        blend(j, 1 - core)
        out_remote(j, core).start()
        blend(j, core)
        out_local(j).start()

    def weigh(j):
        for unit in range(2 * GROUP):
            block, h = unit // GROUP, unit % GROUP
            base = 2 * block
            score = sbuf.at[unit % 2]
            q = qbuf[block, j, :, h * HEAD_DIM:(h + 1) * HEAD_DIM]
            upper = (
                lax.broadcasted_iota(jnp.int32, (tok, tok), 1) > lax.broadcasted_iota(jnp.int32, (tok, tok), 0)
            )
            for i in (4, 0, 1, 2, 3):
                s = lax.dot_general(
                    q, kv[base + i, j, 0], (((1,), (1,)), ((), ())), preferred_element_type=jnp.float32
                )
                if i == 4:
                    last = s
                    continue
                s = jnp.where(4 * row + side + base + i >= 4, s, jnp.float32(-1e30))
                if i == 0:
                    s = jnp.where(upper, s, last)
                score[:, i * tok:(i + 1) * tok] = s
            for r in range(0, tok, TILE):
                part = score[r:r + TILE, :]
                top = jnp.max(part, axis=1, keepdims=True)
                expo = jnp.exp2((part - top) * jnp.float32(SCALE_LOG2E))
                weight = expo * (1.0 / jnp.sum(expo, axis=1, keepdims=True))
                rows_here = slice(h * tok + r, h * tok + r + TILE)
                first = weight[:, :tok]
                ahead = (
                    lax.broadcasted_iota(jnp.int32, (TILE, tok), 1)
                    > lax.broadcasted_iota(jnp.int32, (TILE, tok), 0) + r
                )
                wbuf[block, 0, rows_here, :] = jnp.where(ahead, first, 0.0).astype(wbuf.dtype)
                wbuf[block, 4, rows_here, :] = jnp.where(ahead, 0.0, first).astype(wbuf.dtype)
                for i in range(1, 4):
                    wbuf[block, i, rows_here, :] = weight[:, i * tok:(i + 1) * tok].astype(wbuf.dtype)

    def blend(j, block):
        base = 2 * block
        out = None
        for i in range(5):
            term = jnp.dot(wbuf[block, i], kv[base + i, j, 1], preferred_element_type=jnp.float32)
            out = term if out is None else out + term
        out = out.astype(obuf.dtype)
        for h in range(GROUP):
            obuf[block, j, :, h * HEAD_DIM:(h + 1) * HEAD_DIM] = out[h * tok:(h + 1) * tok]

    def out_local(j):
        return pltpu.make_async_copy(
            obuf.at[core, j], o_ref.at[:, cols(core * HALF_KV + j, GROUP * HEAD_DIM)], osem.at[j]
        )

    def out_remote(j, half):
        return pltpu.make_async_remote_copy(
            src_ref=obuf.at[1 - core, j], dst_ref=o_ref.at[:, cols(half * HALF_KV + j, GROUP * HEAD_DIM)],
            send_sem=osend.at[j], recv_sem=orecv.at[j], device_id=partner, device_id_type=MESH,
        )

    for j in range(HALF_KV):
        for part in (0, 1):
            stage(j, part, core).start()
            stage(j, part, 1 - core).start()
        q_stage(j).start()

    barrier = pltpu.get_barrier_semaphore()
    for device in (partner, side_same, side_cross):
        pl.semaphore_signal(barrier, inc=1, device_id=device, device_id_type=MESH)

    @pl.when(has_next)
    def _():
        for device in (next_same, next_cross):
            pl.semaphore_signal(barrier, inc=1, device_id=device, device_id_type=MESH)

    @pl.when(has_prev)
    def _():
        for device in (prev_same, prev_cross):
            pl.semaphore_signal(barrier, inc=1, device_id=device, device_id_type=MESH)

    @pl.when(jnp.logical_not(has_prev))
    def _():
        kv[0:3] = jnp.zeros((3,) + kv.shape[1:], kv.dtype)

        @pl.when(side == 0)
        def _():
            kv[3] = jnp.zeros(kv.shape[1:], kv.dtype)

    pl.semaphore_wait(barrier, 3 + jnp.where(has_next, 2, 0) + jnp.where(has_prev, 2, 0))

    for j, part in ((0, 0), (0, 1), (1, 0)):
        staged(j, part)
        direct_next(j, part, launch)
        direct_side(j, part, launch)
        if part == 0:
            q_swap(j, core).start()
    for j, part in ((1, 1), (2, 0), (2, 1), (3, 0), (3, 1)):
        staged(j, part)
        if part == 0:
            q_swap(j, core).start()

    @pl.when(side == 1)
    def _():
        direct_side(1, 1, launch)
        direct_side(2, 0, launch)

    def step(j, carry):
        @pl.when(j < HALF_KV)
        def _():
            exchange(j, 0)

        @pl.when(j > 0)
        def _():
            weigh_chunk(j - 1)

        @pl.when(j < HALF_KV)
        def _():
            exchange(j, 1)

        @pl.when(j > 0)
        def _():
            blend_chunk(j - 1)

        return carry

    lax.fori_loop(0, HALF_KV + 1, step, 0)

    def finish(j, carry):
        q_swap(j, core).wait_send()
        for part in (0, 1):
            forwards(j, part, lambda copy, slot: None if copy is None else copy.wait_send())
        out_local(j).wait()
        out_remote(j, core).wait_send()
        out_remote(j, 1 - core).wait_recv()
        return carry

    lax.fori_loop(0, HALF_KV, finish, 0)


def fused_body(rows, queries, keys, values):
    tok = queries.shape[0]
    kind = queries.dtype
    wide = GROUP * HEAD_DIM
    dma = pltpu.SemaphoreType.DMA
    return pl.pallas_call(
        functools.partial(fused_kernel, rows),
        out_shape=jax.ShapeDtypeStruct(queries.shape, kind),
        in_specs=[pl.BlockSpec(memory_space=pl.ANY)] * 3,
        out_specs=pl.BlockSpec(memory_space=pl.ANY),
        scratch_shapes=[
            pltpu.VMEM((SLOTS, HALF_KV, 2, tok, HEAD_DIM), kind),
            pltpu.VMEM((HALF_KV, 2, tok, HEAD_DIM), kind),
            pltpu.VMEM((2, HALF_KV, tok, wide), kind),
            pltpu.VMEM((2, tok, WINDOW), jnp.float32),
            pltpu.VMEM((2, 5, GROUP * tok, tok), kind),
            pltpu.VMEM((2, HALF_KV, tok, wide), kind),
            dma((HALF_KV, 4)),
            dma((HALF_KV,)),
            dma((HALF_KV,)),
            dma((HALF_KV,)),
            dma((8, HALF_KV, 2)),
            dma((SLOTS, HALF_KV, 2)),
            dma((HALF_KV,)),
            dma((HALF_KV,)),
            dma((HALF_KV,)),
        ],
        compiler_params=pltpu.CompilerParams(
            collective_id=0, has_side_effects=True, vmem_limit_bytes=40 * 1024 * 1024
        ),
        cost_estimate=pl.CostEstimate(
            flops=4 * tok * HEADS * HEAD_DIM * (WINDOW + tok), bytes_accessed=6 * tok * HEADS * HEAD_DIM,
            transcendentals=tok * HEADS * WINDOW,
        ),
        name="window_attention",
    )(*(pltpu.with_memory_space_constraint(x, pltpu.HBM) for x in (queries, keys, values)))


def from_behind(x, axis, by):
    peers = lax.axis_size(axis)
    pairs = [(i, i + by) for i in range(peers) if 0 <= i + by < peers]
    return lax.ppermute(x, axis, pairs)


def attend_block(query_rows, key_win, value_win, block_index):
    tok_rows = query_rows.shape[0]
    span_rows = key_win.shape[0]
    row_ids = jnp.arange(tok_rows, dtype=jnp.int32)[:, None]
    col_ids = jnp.arange(span_rows, dtype=jnp.int32)[None, :]
    position = block_index * tok_rows - WINDOW + col_ids
    allowed = (col_ids > row_ids) & (col_ids <= row_ids + WINDOW) & (position >= 0)

    def head_group(head_index):
        query_part = lax.dynamic_slice_in_dim(query_rows, head_index * GROUP * HEAD_DIM, GROUP * HEAD_DIM, 1)
        query_part = query_part.reshape(tok_rows, GROUP, HEAD_DIM)
        key_part = lax.dynamic_slice_in_dim(key_win, head_index * HEAD_DIM, HEAD_DIM, 1)
        value_part = lax.dynamic_slice_in_dim(value_win, head_index * HEAD_DIM, HEAD_DIM, 1)
        score = jnp.einsum(
            "thd,kd->htk", query_part, key_part, preferred_element_type=jnp.float32
        ) * HEAD_DIM ** (-0.5)
        score = jnp.where(allowed[None], score, jnp.float32(-1e30))
        largest = jnp.max(score, axis=2, keepdims=True)
        expo = jnp.where(allowed[None], jnp.exp(score - largest), jnp.float32(0.0))
        total = jnp.sum(expo, axis=2, keepdims=True)
        weight = (expo / total).astype(jnp.bfloat16)
        output = jnp.einsum("htk,kd->thd", weight, value_part, preferred_element_type=jnp.float32)
        return output.astype(jnp.bfloat16).reshape(tok_rows, GROUP * HEAD_DIM)

    parts = lax.map(head_group, jnp.arange(KV_HEADS, dtype=jnp.int32))
    return jnp.transpose(parts, (1, 0, 2)).reshape(tok_rows, HEADS * HEAD_DIM)


def plain_body(queries, keys, values):
    back_blocks = WINDOW // queries.shape[0]
    block_index = lax.axis_index(("blk", "grp"))
    pieces_k = []
    pieces_v = []
    for offset in range(back_blocks, 0, -1):
        moved_k, moved_v = from_behind((keys, values), ("blk", "grp"), offset)
        pieces_k.append(moved_k)
        pieces_v.append(moved_v)
    key_win = jnp.concatenate(pieces_k + [keys], axis=0)
    value_win = jnp.concatenate(pieces_v + [values], axis=0)
    return attend_block(queries, key_win, value_win, block_index)


def solution(mesh):
    blks, grps = mesh.shape["blk"], mesh.shape["grp"]
    placed = P(("blk", "grp"), None)

    def body(queries, keys, values):
        if grps == 2 and blks % 2 == 0 and 4 * queries.shape[0] == WINDOW:
            return fused_body(blks // 2, queries, keys, values)
        return plain_body(queries, keys, values)

    return jax.shard_map(
        body, mesh=mesh, in_specs=(placed, placed, placed), out_specs=placed, check_vma=False
    )
```
